256 devices in a mesh: depth: 4 (over z_lo, core), scan: 64 (over z_hi, x, y).
Axes of the slice: x: 4, y: 4, z: 8 (z_hi: 4, z_lo: 2; z = z_hi * 2 + z_lo), core: 2. Of those that a mesh axis runs over, the one named last changes fastest.
Arguments:
- transmission: float32 [4, 2, 4096, 3072], P('depth', None, 'scan'), may hold values from -5 to 5
- probe: float32 [2, 256, 256], replicated, may hold values from -6 to 6
- exit_adjoint: float32 [2, 128, 2, 256, 256], P(None, 'scan'), may hold values from -6 to 6
- scan_row: int32 [2, 128], P(None, 'scan'), may hold values from 0 to 4095, as said below
- scan_col: int32 [2, 128], P(None, 'scan'), may hold values from 0 to 2816
Outputs:
- object_grad: float32 [4, 2, 4096, 3072], P('depth', None, 'scan')
- probe_grad: float32 [2, 256, 256], P(None, 'depth')
The draws below stay inside these ranges and needn't reach their ends.
Inputs may be any that keep to these rules, and one draw needn't show every extreme that they name: `scan_row`: entries 2 * j to 2 * (j + 1) - 1 of every batch lie in rows 64 * j to 64 * (j + 1) - 1: they are the positions of scan region j.
All inputs are finite; a program needn't handle non-finite values.
Results may differ from the reference program's by a relative error of at most 0.0075.
Values may be sent and summed in bfloat16 or wider, within the bound.
A program may use at most 128 MiB of HBM per device.

```python
import math
import jax
import jax.numpy as jnp
from jax import lax

P_SIZE = 256
STRIP = 64
W = 3072
S_DEV = 1
NB = 2
POS_DEV = 2
NSL = 4
ROWS = 4096
POSITIONS = 128


def draw_scan_row(key, part):
    key = jax.random.fold_in(key, 7)
    offset_key, first_key, last_key = jax.random.split(key, 3)
    offsets = jax.random.randint(offset_key, (NB, POSITIONS), 0, STRIP)
    regions = (jnp.arange(POSITIONS) // POS_DEV)[None, :]
    row_values = offsets + regions * STRIP
    first_pick = jax.random.randint(first_key, (), 0, POS_DEV)
    last_pick = jax.random.randint(last_key, (), 0, POS_DEV)
    row_values = row_values.at[0, first_pick].set(0)
    row_values = row_values.at[NB - 1, POSITIONS - POS_DEV + last_pick].set(ROWS - 1)
    return row_values.astype(jnp.int32)


def draw_scan_col(key, part):
    key = jax.random.fold_in(key, 13)
    value_key, low_key, high_key = jax.random.split(key, 3)
    col_values = jax.random.randint(value_key, (NB * POSITIONS,), 0, W - P_SIZE + 1)
    low_pick = jax.random.randint(low_key, (), 0, NB * POSITIONS // 2)
    high_pick = jax.random.randint(high_key, (), NB * POSITIONS // 2, NB * POSITIONS)
    col_values = col_values.at[low_pick].set(0)
    col_values = col_values.at[high_pick].set(W - P_SIZE)
    return col_values.reshape(NB, POSITIONS).astype(jnp.int32)


def block_scale(own_key, shape, cuts, low, largest):
    gain = 1.0
    for position, shards_of in cuts:
        draws = jax.random.uniform(jax.random.fold_in(jax.random.fold_in(own_key, 6), position), (shards_of,), jnp.float32, low / len(cuts), largest / len(cuts))
        gain = gain * jnp.repeat(jnp.exp(draws), shape[position] // shards_of).reshape((-1,) + (1,) * (len(shape) - 1 - position))
    return gain


def noise(key, shape, scale, reach, cuts=(), held_as=jnp.bfloat16):
    result = scale * jax.random.normal(key, shape, jnp.float32)
    if cuts:
        result = result * block_scale(key, shape, cuts, -0.22, 0.18)
    return jnp.clip(result, -reach, reach).astype(held_as)


def setup_inputs(seed: int = 0) -> dict:
    streams_of = jax.random.split(jax.random.key(seed), 6)
    transmission = noise(streams_of[0], (NSL, 2, ROWS, W), 0.7, 5.0, ((0, 4), (2, 64)), jnp.float32)
    probe = noise(streams_of[1], (2, P_SIZE, P_SIZE), 1.0, 6.0, (), jnp.float32)
    exit_adjoint = noise(streams_of[2], (NB, POSITIONS, 2, P_SIZE, P_SIZE), 1.0, 6.0, ((1, 64),), jnp.float32)
    scan_row = draw_scan_row(jax.random.fold_in(streams_of[5], 71), 0)
    scan_col = draw_scan_col(jax.random.fold_in(streams_of[5], 71), 0)
    return {"transmission": transmission, "probe": probe, "exit_adjoint": exit_adjoint, "scan_row": scan_row, "scan_col": scan_col}


fresnel = 0.25


def transfer(extent):
    indices = jnp.arange(extent)
    frequency = jnp.where(indices < extent // 2, indices, indices - extent).astype(jnp.float32)
    phases = (-math.pi * fresnel / extent) * frequency * frequency
    factor = lax.complex(jnp.cos(phases), jnp.sin(phases))
    return factor[:, None] * factor[None, :]


def propagate(fields, spectrum):
    return jnp.fft.ifft2(jnp.fft.fft2(fields) * spectrum)


def rounded(values):
    real_part = lax.optimization_barrier(jnp.real(values).astype(jnp.bfloat16)).astype(jnp.float32)
    imag_part = lax.optimization_barrier(jnp.imag(values).astype(jnp.bfloat16)).astype(jnp.float32)
    return lax.complex(real_part, imag_part)


def reference(transmission, probe, exit_adjoint, scan_row, scan_col):
    forward_kernel = transfer(P_SIZE)
    backward_kernel = jnp.conj(forward_kernel)
    extended = jnp.concatenate([transmission, transmission[:, :, :P_SIZE, :]], axis=2)
    probe_c = lax.complex(probe[0], probe[1])
    adjoints = lax.complex(exit_adjoint[:, :, 0], exit_adjoint[:, :, 1]).reshape(NB * POSITIONS, P_SIZE, P_SIZE)
    all_rows = scan_row.reshape(-1).astype(jnp.int32)
    all_cols = scan_col.reshape(-1).astype(jnp.int32)
    zero_index = jnp.zeros((), jnp.int32)

    def visit(carry_pair, inputs_now):
        gradient, probe_total = carry_pair
        row_start, col_start, adjoint_now = inputs_now
        anchor = (zero_index, zero_index, row_start, col_start)
        patch_block = lax.dynamic_slice(extended, anchor, (NSL, 2, P_SIZE, P_SIZE))
        patches = lax.complex(patch_block[:, 0], patch_block[:, 1])
        current = probe_c
        incident = []
        for layer in range(NSL):
            if layer > 0 and layer % S_DEV == 0:
                current = rounded(current)
            incident.append(current)
            current = propagate(patches[layer] * current, forward_kernel)
        updates = []
        current = adjoint_now
        for layer in reversed(range(NSL)):
            if layer + 1 < NSL and (layer + 1) % S_DEV == 0:
                current = rounded(current)
            spread_back = propagate(current, backward_kernel)
            updates.append(jnp.conj(incident[layer]) * spread_back)
            current = jnp.conj(patches[layer]) * spread_back
        update = jnp.stack(updates[::-1])
        update = jnp.stack([jnp.real(update), jnp.imag(update)], axis=1)
        before = lax.dynamic_slice(gradient, anchor, (NSL, 2, P_SIZE, P_SIZE))
        gradient = lax.dynamic_update_slice(gradient, before + update, anchor)
        return (gradient, probe_total + current), None

    start_grad = jnp.zeros((NSL, 2, ROWS + P_SIZE, W), jnp.float32)
    start_probe = lax.complex(jnp.zeros((P_SIZE, P_SIZE), jnp.float32), jnp.zeros((P_SIZE, P_SIZE), jnp.float32))
    (gradient, probe_total), _ = lax.scan(visit, (start_grad, start_probe), (all_rows, all_cols, adjoints))
    object_grad = gradient[:, :, :ROWS, :].at[:, :, :P_SIZE, :].add(gradient[:, :, ROWS:, :])
    probe_grad = jnp.stack([jnp.real(probe_total), jnp.imag(probe_total)])
    return object_grad, probe_grad
```

```python
import functools
import math

import jax
import jax.numpy as jnp
import numpy as np
from jax import lax
from jax.experimental import pallas as pl
from jax.experimental.pallas import tpu as pltpu
from jax.sharding import PartitionSpec as P

FRESNEL = 0.25
SIDE = 256
HALF = SIDE // 2
STRIP = 64
RIM = SIDE // STRIP
BATCHES = 2
PER = 2
F32 = jnp.float32
BF16 = jnp.bfloat16
MESH = pl.DeviceIdType.MESH


def tables():
    k = np.arange(SIDE)
    f = np.where(k < HALF, k, k - SIDE).astype(np.float64)
    h = np.exp(-1j * math.pi * FRESNEL * f * f / SIDE)
    dft = np.exp(-2j * math.pi * (np.outer(k, k) % SIDE) / SIDE)
    a = (dft.conj() / SIDE) @ (h[:, None] * dft)
    lefts, rights = [], []
    for sign in (1.0, -1.0):
        m = (a[:HALF, :HALF] + sign * a[:HALF, HALF:]) / 2.0
        left = np.block([[m.real, -m.imag], [m.imag, m.real]]).astype(np.float32)
        for out, full in ((lefts, left), (rights, left.T.copy())):
            high = full.astype(jnp.bfloat16)
            low = (full - high.astype(np.float32)).astype(jnp.bfloat16)
            out.append(np.stack([high, low]))
    return np.stack([np.stack(lefts), np.stack(rights)])


def dot(a, b):
    return jnp.dot(a, b, preferred_element_type=F32)


def split(x):
    high = x.astype(BF16)
    return high, (x - high.astype(F32)).astype(BF16)


def propagate(x_ref, w_ref, tab):
    middle = []
    for a in range(2):
        parts = []
        for ri in range(2):
            top, low = x_ref[ri, :HALF, :], x_ref[ri, HALF:, :]
            v = top + low if a == 0 else top - low
            l, r = v[:, :HALF], v[:, HALF:]
            parts.append(jnp.concatenate([l + r, l - r], axis=1))
        high, low = split(jnp.concatenate(parts, axis=0))
        left_high, left_low = tab[0, a, 0], tab[0, a, 1]
        middle.append(dot(left_high, high) + dot(left_low, high) + dot(left_high, low))
    sectors = []
    for b in range(2):
        cols = slice(b * HALF, (b + 1) * HALF)
        rows = [jnp.concatenate([z[:HALF, cols], z[HALF:, cols]], axis=1) for z in middle]
        high, low = split(jnp.concatenate(rows, axis=0))
        right_high, right_low = tab[1, b, 0], tab[1, b, 1]
        sectors.append(dot(high, right_high) + dot(high, right_low) + dot(low, right_high))
    for ri in range(2):
        cols = slice(ri * HALF, (ri + 1) * HALF)
        for half_col in range(2):
            s, d = sectors[0][:, cols], sectors[1][:, cols]
            v = s + d if half_col == 0 else s - d
            out = slice(half_col * HALF, (half_col + 1) * HALF)
            w_ref[ri, :HALF, out] = v[:HALF] + v[HALF:]
            w_ref[ri, HALF:, out] = v[:HALF] - v[HALF:]


def times(ar, ai, br, bi):
    return ar * br - ai * bi, ar * bi + ai * br


def main_kernel(
    group, hi_count, n_scan,
    trans, probe, exit_adjoint, table_in, idx_in,
    pieces, idx_all, probe_out,
    strip, tab, probe_v, exit_v, idx_s,
    sbuf, tbuf, x_v, start_v, w1_v, w2_v, w3_v, w4_v, zsend, zrecv,
    gbuf, total_v, part_s, part_r, rs_s, rs_r, ar_s, ar_r,
    local_sems, strip_sems, idx_send, idx_recv, t_send, t_recv, z_send, z_recv,
    g_send, g_recv, p_send, p_recv, rs_send, rs_recv, ar_send, ar_recv, ag_send, ag_recv,
):
    q = lax.axis_index("depth")
    j = lax.axis_index("scan")
    z = q // 2
    c = q % 2
    member = j % group
    level = j // group

    def at(depth, scan):
        return {"depth": depth, "scan": scan}

    def region(step):
        return lax.rem(j + step + n_scan, n_scan)

    def mate(i):
        return level * group + lax.rem(member + i, group)

    def tier(i):
        return lax.rem(level + i, hi_count) * group + member

    loads = [
        pltpu.make_async_copy(table_in, tab, local_sems.at[1]),
        pltpu.make_async_copy(probe, probe_v, local_sems.at[2]),
        pltpu.make_async_copy(exit_adjoint.at[c], exit_v, local_sems.at[3]),
        pltpu.make_async_copy(idx_in, idx_all.at[0], local_sems.at[4]),
    ]

    def strip_copy(i):
        cols = pl.ds(pl.multiple_of(i * HALF, HALF), HALF)
        return pltpu.make_async_copy(trans.at[0, :, :, cols], strip.at[i], strip_sems.at[i])

    for copy in loads:
        copy.start()

    def start_strip(i, carry):
        strip_copy(i).start()
        return carry

    def wait_strip(i, carry):
        strip_copy(i).wait()
        return carry

    lax.fori_loop(0, strip.shape[0], start_strip, 0)

    barrier = pltpu.get_barrier_semaphore()
    partners = [at(q + 1 - 2 * c, j), at(q + 2 - 4 * z, j), at(3 - q, j)]
    for d in range(1, RIM + 1):
        for b in range(2):
            partners.append(at(2 * z + b, region(d)))
            partners.append(at(2 * z + b, region(-d)))
    for i in range(1, group):
        partners.append(at(q, mate(i)))
    for i in range(1, hi_count):
        partners.append(at(q, tier(i)))
    for device in partners:
        pl.semaphore_signal(barrier, inc=1, device_id=device, device_id_type=MESH)
    pl.semaphore_wait(barrier, len(partners))

    idx_copies = [
        pltpu.make_async_remote_copy(
            src_ref=idx_in, dst_ref=idx_all.at[d], send_sem=idx_send.at[d], recv_sem=idx_recv.at[d],
            device_id=at(q, region(d)), device_id_type=MESH)
        for d in range(1, RIM + 1)
    ]
    for copy in idx_copies:
        copy.start()
    loads[3].wait()
    for copy in idx_copies:
        copy.wait_recv()
    to_smem = pltpu.make_async_copy(idx_all, idx_s, local_sems.at[5])
    to_smem.start()
    to_smem.wait()
    lax.fori_loop(0, strip.shape[0], wait_strip, 0)

    lane = lax.broadcasted_iota(jnp.int32, (1, 1, HALF), 2)
    last_block = strip.shape[0] - 1

    def t_copy(k, d, b):
        return pltpu.make_async_remote_copy(
            src_ref=sbuf.at[k, d, b], dst_ref=tbuf.at[k, c, d],
            send_sem=t_send.at[k, d, b], recv_sem=t_recv.at[k, c, d],
            device_id=at(2 * z + b, region(-d)), device_id_type=MESH)

    def t_sibling(k):
        return pltpu.make_async_remote_copy(
            src_ref=sbuf.at[k, 0, 1 - c], dst_ref=tbuf.at[k, c, 0],
            send_sem=t_send.at[k, 0, 1], recv_sem=t_recv.at[k, c, 0],
            device_id=at(q + 1 - 2 * c, j), device_id_type=MESH)

    def t_local(k):
        return pltpu.make_async_copy(sbuf.at[k, 0, c], tbuf.at[k, c, 0], t_send.at[k, 0, 0])

    def t_arrival(k, slot, d):
        return pltpu.make_async_remote_copy(
            src_ref=sbuf.at[k, d, 0], dst_ref=tbuf.at[k, slot, d],
            send_sem=t_send.at[k, d, 0], recv_sem=t_recv.at[k, slot, d],
            device_id=at(q + 1 - 2 * c, j), device_id_type=MESH)

    def send_windows(k, carry):
        for d in (4, 3, 2, 1, 0):
            for b in range(2):
                col = idx_s[d, 0, 4 + 2 * b + k]
                block = lax.shift_right_logical(col, 7)
                offset = col & (HALF - 1)
                first, second = strip[block], strip[block + 1]
                third = strip[jnp.minimum(block + 2, last_block)]
                sbuf[k, d, b, :, :, :HALF] = jnp.where(lane >= offset, first, third).astype(BF16)
                sbuf[k, d, b, :, :, HALF:] = second.astype(BF16)
                if d > 0:
                    t_copy(k, d, b).start()
        t_sibling(k).start()
        t_local(k).start()
        return carry

    lax.fori_loop(0, PER, send_windows, 0)

    def wait_windows(k):
        for d in (0, 1, 2, 3, 4):
            if d == 0:
                t_local(k).wait()
                t_arrival(k, 1 - c, 0).wait_recv()
            else:
                for slot in range(2):
                    t_arrival(k, slot, d).wait_recv()

    row = lax.broadcasted_iota(jnp.int32, (STRIP, 1), 0)

    def offsets(k):
        e = 2 * c + k
        return idx_s[0, 0, e] & (STRIP - 1), idx_s[0, 0, 4 + e] & (HALF - 1)

    def window(k, slot, block, row_offset):
        if block > 0:
            return tbuf[k, slot, block, 0].astype(F32), tbuf[k, slot, block, 1].astype(F32)
        here = row >= row_offset
        return tuple(
            jnp.where(here, tbuf[k, slot, 0, ri].astype(F32), tbuf[k, slot, RIM, ri].astype(F32))
            for ri in range(2)
        )

    blocks = [slice(i * STRIP, (i + 1) * STRIP) for i in range(RIM)]

    def roll(x, rows, cols):
        return pltpu.roll(pltpu.roll(x, rows, 0), cols, 1)

    def z_copy(k):
        return pltpu.make_async_remote_copy(
            src_ref=zsend.at[k], dst_ref=zrecv.at[k], send_sem=z_send.at[k], recv_sem=z_recv.at[k],
            device_id=at(q + 2 - 4 * z, j), device_id_type=MESH)

    for copy in loads[:3]:
        copy.wait()

    def first_half(k, carry):
        row_offset, col_offset = offsets(k)

        @pl.when(z == 0)
        def _():
            for ri in range(2):
                start_v[k, ri] = roll(probe_v[ri], row_offset, col_offset)
            wait_windows(k)
            for i, rows in enumerate(blocks):
                tr, ti = window(k, 0, i, row_offset)
                x_v[0, rows, :], x_v[1, rows, :] = times(tr, ti, start_v[k, 0, rows, :], start_v[k, 1, rows, :])

        @pl.when(z == 1)
        def _():
            x_v[0] = roll(exit_v[k, 0], row_offset, col_offset)
            x_v[1] = -roll(exit_v[k, 1], row_offset, col_offset)

        propagate(x_v, w1_v.at[k], tab)

        @pl.when(z == 1)
        def _():
            wait_windows(k)

        for i, rows in enumerate(blocks):
            tr, ti = window(k, 1, i, row_offset)
            x_v[0, rows, :], x_v[1, rows, :] = times(tr, ti, w1_v[k, 0, rows, :], w1_v[k, 1, rows, :])
        propagate(x_v, w2_v.at[k], tab)

        @pl.when(z == 0)
        def _():
            zsend[k] = w2_v[k].astype(BF16)

        @pl.when(z == 1)
        def _():
            for i, rows in enumerate(blocks):
                tr, ti = window(k, 0, i, row_offset)
                vr, vi = times(tr, ti, w2_v[k, 0, rows, :], w2_v[k, 1, rows, :])
                zsend[k, 0, rows, :] = vr.astype(BF16)
                zsend[k, 1, rows, :] = vi.astype(BF16)

        z_copy(k).start()
        return carry

    lax.fori_loop(0, PER, first_half, 0)

    def g_copy(k, slot, d):
        return pltpu.make_async_remote_copy(
            src_ref=gbuf.at[k, slot, d % RIM], dst_ref=pieces.at[k, c, d],
            send_sem=g_send.at[k, slot, d], recv_sem=g_recv.at[k, c, d],
            device_id=at(2 * z + slot, region(d)), device_id_type=MESH)

    def g_sibling(k):
        return pltpu.make_async_remote_copy(
            src_ref=gbuf.at[k, 1 - c, 0], dst_ref=pieces.at[k, c, 0],
            send_sem=g_send.at[k, 1, 0], recv_sem=g_recv.at[k, c, 0],
            device_id=at(q + 1 - 2 * c, j), device_id_type=MESH)

    def g_local(k):
        return pltpu.make_async_copy(gbuf.at[k, c, 0], pieces.at[k, c, 0], g_send.at[k, 0, 0])

    def g_arrival(k, core, d):
        return pltpu.make_async_remote_copy(
            src_ref=gbuf.at[k, 0, d % RIM], dst_ref=pieces.at[k, core, d],
            send_sem=g_send.at[k, 0, d], recv_sem=g_recv.at[k, core, d],
            device_id=at(q + 1 - 2 * c, j), device_id_type=MESH)

    def second_half(k, carry):
        row_offset, col_offset = offsets(k)
        z_copy(k).wait_recv()

        @pl.when(z == 0)
        def _():
            x_v[...] = zrecv[k].astype(F32)

        @pl.when(z == 1)
        def _():
            for i, rows in enumerate(blocks):
                tr, ti = window(k, 0, i, row_offset)
                vr, vi = zrecv[k, 0, rows, :].astype(F32), zrecv[k, 1, rows, :].astype(F32)
                x_v[0, rows, :], x_v[1, rows, :] = times(tr, ti, vr, vi)
                gr, gi = times(vr, vi, w2_v[k, 0, rows, :], w2_v[k, 1, rows, :])
                gbuf[k, 0, i, 0] = gr.astype(BF16)
                gbuf[k, 0, i, 1] = (-gi).astype(BF16)

        propagate(x_v, w3_v, tab)
        for i, rows in enumerate(blocks):
            gr, gi = times(w1_v[k, 0, rows, :], w1_v[k, 1, rows, :], w3_v[0, rows, :], w3_v[1, rows, :])
            gbuf[k, 1, i, 0] = gr.astype(BF16)
            gbuf[k, 1, i, 1] = (-gi).astype(BF16)
        for d in (4, 3, 2, 1):
            g_copy(k, 1, d).start()

        @pl.when(z == 0)
        def _():
            for i, rows in enumerate(blocks):
                tr, ti = window(k, 1, i, row_offset)
                x_v[0, rows, :], x_v[1, rows, :] = times(tr, ti, w3_v[0, rows, :], w3_v[1, rows, :])
            propagate(x_v, w4_v, tab)
            for i, rows in enumerate(blocks):
                wr, wi = w4_v[0, rows, :], w4_v[1, rows, :]
                gr, gi = times(start_v[k, 0, rows, :], start_v[k, 1, rows, :], wr, wi)
                gbuf[k, 0, i, 0] = gr.astype(BF16)
                gbuf[k, 0, i, 1] = (-gi).astype(BF16)

        for d in (4, 3, 2, 1):
            g_copy(k, 0, d).start()
        g_sibling(k).start()
        g_local(k).start()

        @pl.when(z == 0)
        def _():
            for i, rows in enumerate(blocks):
                tr, ti = window(k, 0, i, row_offset)
                vr, vi = times(tr, ti, w4_v[0, rows, :], w4_v[1, rows, :])
                x_v[0, rows, :], x_v[1, rows, :] = vr, -vi
            back_rows, back_cols = (SIDE - row_offset) & (SIDE - 1), (SIDE - col_offset) & (SIDE - 1)
            for ri in range(2):
                moved = roll(x_v[ri], back_rows, back_cols)
                total_v[ri] = jnp.where(k > 0, total_v[ri], 0.0) + moved

        return carry

    lax.fori_loop(0, PER, second_half, 0)

    def p_copy(section):
        return pltpu.make_async_remote_copy(
            src_ref=part_s.at[section], dst_ref=part_r.at[c], send_sem=p_send.at[section],
            recv_sem=p_recv.at[c], device_id=at(section, j), device_id_type=MESH)

    def p_arrival(core):
        return pltpu.make_async_remote_copy(
            src_ref=part_s.at[0], dst_ref=part_r.at[core], send_sem=p_send.at[0],
            recv_sem=p_recv.at[core], device_id=at(q + 1 - 2 * c, j), device_id_type=MESH)

    @pl.when(z == 0)
    def _():
        for section in range(4):
            part_s[section] = total_v[:, section * STRIP:(section + 1) * STRIP, :].astype(BF16)
        p_copy(2).start()
        p_copy(3).start()
        p_copy(1 - c).start()
        own = pltpu.make_async_copy(part_s.at[c], part_r.at[c], p_send.at[c])
        own.start()
        own.wait()
        p_arrival(1 - c).wait_recv()

    @pl.when(z == 1)
    def _():
        p_arrival(0).wait_recv()
        p_arrival(1).wait_recv()

    block_sum = part_r[0].astype(F32) + part_r[1].astype(F32)
    rs_s[...] = block_sum.reshape(rs_s.shape)

    def rs_copy(i):
        target = lax.rem(member + i, group)
        return pltpu.make_async_remote_copy(
            src_ref=rs_s.at[target], dst_ref=rs_r.at[member], send_sem=rs_send.at[i],
            recv_sem=rs_recv.at[i], device_id=at(q, mate(i)), device_id_type=MESH)

    for i in range(1, group):
        rs_copy(i).start()
    rs_r[member] = rs_s[member]
    for i in range(1, group):
        rs_copy(i).wait_recv()
    piece_sum = rs_r[0]
    for m in range(1, group):
        piece_sum = piece_sum + rs_r[m]
    ar_s[...] = piece_sum
    ar_r[level] = piece_sum

    def ar_copy(i):
        return pltpu.make_async_remote_copy(
            src_ref=ar_s, dst_ref=ar_r.at[level], send_sem=ar_send.at[i],
            recv_sem=ar_recv.at[i], device_id=at(q, tier(i)), device_id_type=MESH)

    for i in range(1, hi_count):
        ar_copy(i).start()
    for i in range(1, hi_count):
        ar_copy(i).wait()
    piece_sum = ar_r[0]
    for m in range(1, hi_count):
        piece_sum = piece_sum + ar_r[m]
    probe_out[member] = piece_sum

    def ag_copy(i):
        return pltpu.make_async_remote_copy(
            src_ref=probe_out.at[member], dst_ref=probe_out.at[member], send_sem=ag_send.at[i],
            recv_sem=ag_recv.at[i], device_id=at(q, mate(i)), device_id_type=MESH)

    for i in range(1, group):
        ag_copy(i).start()
    for i in range(1, group):
        ag_copy(i).wait()

    for copy in idx_copies:
        copy.wait_send()
    for i in range(1, group):
        rs_copy(i).wait_send()

    @pl.when(z == 0)
    def _():
        p_copy(2).wait_send()
        p_copy(3).wait_send()
        p_copy(1 - c).wait_send()

    def drain(k, carry):
        z_copy(k).wait_send()
        t_sibling(k).wait_send()
        g_sibling(k).wait_send()
        g_local(k).wait()
        g_arrival(k, 1 - c, 0).wait_recv()
        for d in range(1, RIM + 1):
            for b in range(2):
                t_copy(k, d, b).wait_send()
                g_copy(k, b, d).wait_send()
                g_arrival(k, b, d).wait_recv()
        return carry

    lax.fori_loop(0, PER, drain, 0)


def main_call(transmission, probe, exit_adjoint, idx):
    n_scan = lax.axis_size("scan")
    group = 16 if n_scan % 16 == 0 else 4
    hi_count = n_scan // group
    piece = (16 // group, 8, SIDE)
    any_spec = pl.BlockSpec(memory_space=pl.ANY)
    vmem_spec = pl.BlockSpec(memory_space=pltpu.VMEM)
    field = (2, SIDE, SIDE)
    dma = pltpu.SemaphoreType.DMA
    columns = transmission.shape[3]
    return pl.pallas_call(
        functools.partial(main_kernel, group, hi_count, n_scan),
        out_shape=(
            jax.ShapeDtypeStruct((PER, 2, RIM + 1, 2, STRIP, SIDE), BF16),
            jax.ShapeDtypeStruct((RIM + 1, 8, 128), jnp.int32),
            jax.ShapeDtypeStruct((group,) + piece, F32),
        ),
        in_specs=[any_spec] * 5,
        out_specs=(any_spec, any_spec, vmem_spec),
        scratch_shapes=[
            pltpu.VMEM((columns // HALF, 2, STRIP, HALF), F32),
            pltpu.VMEM((2, 2, 2, SIDE, SIDE), BF16),
            pltpu.VMEM(field, F32),
            pltpu.VMEM((PER,) + field, F32),
            pltpu.SMEM((RIM + 1, 8, 128), jnp.int32),
            pltpu.VMEM((PER, RIM + 1, 2, 2, STRIP, SIDE), BF16),
            pltpu.VMEM((PER, 2, RIM + 1, 2, STRIP, SIDE), BF16),
            pltpu.VMEM(field, F32),
            pltpu.VMEM((PER,) + field, F32),
            pltpu.VMEM((PER,) + field, F32),
            pltpu.VMEM((PER,) + field, F32),
            pltpu.VMEM(field, F32),
            pltpu.VMEM(field, F32),
            pltpu.VMEM((PER,) + field, BF16),
            pltpu.VMEM((PER,) + field, BF16),
            pltpu.VMEM((PER, 2, RIM, 2, STRIP, SIDE), BF16),
            pltpu.VMEM(field, F32),
            pltpu.VMEM((4, 2, STRIP, SIDE), BF16),
            pltpu.VMEM((2, 2, STRIP, SIDE), BF16),
            pltpu.VMEM((group,) + piece, F32),
            pltpu.VMEM((group,) + piece, F32),
            pltpu.VMEM(piece, F32),
            pltpu.VMEM((hi_count,) + piece, F32),
            dma((6,)),
            dma((columns // HALF,)),
            dma((RIM + 1,)),
            dma((RIM + 1,)),
            dma((PER, RIM + 1, 2)),
            dma((PER, 2, RIM + 1)),
            dma((PER,)),
            dma((PER,)),
            dma((PER, 2, RIM + 1)),
            dma((PER, 2, RIM + 1)),
            dma((4,)),
            dma((2,)),
            dma((group,)),
            dma((group,)),
            dma((hi_count,)),
            dma((hi_count,)),
            dma((group,)),
            dma((group,)),
        ],
        compiler_params=pltpu.CompilerParams(
            collective_id=0, has_side_effects=True, vmem_limit_bytes=48 * 1024 * 1024
        ),
        cost_estimate=pl.CostEstimate(flops=8 * 12 * 2 * SIDE**3, bytes_accessed=8 << 20, transcendentals=0),
        name="waves",
    )(transmission, probe, exit_adjoint, jnp.asarray(tables()), idx)


def deposit_kernel(idx, pieces, probe_in, grad, probe_out):
    probe_out[...] = probe_in[...]
    grad[...] = jnp.zeros_like(grad)
    lane = lax.broadcasted_iota(jnp.int32, (1, 1, HALF), 2)
    row = lax.broadcasted_iota(jnp.int32, (1, STRIP, 1), 1)

    def add(n, carry):
        d = n // 4
        core = (n // 2) % 2
        k = n % 2
        e = 2 * core + k
        row_offset = idx[d, 0, e] & (STRIP - 1)
        col = idx[d, 0, 4 + e]
        block = lax.shift_right_logical(col, 7)
        col_offset = col & (HALF - 1)
        low = jnp.where(d == 0, row_offset, 0)
        high = jnp.where(d == RIM, row_offset, STRIP)
        keep = (row >= low) & (row < high)
        piece = jnp.where(keep, pieces[k, core, d].astype(F32), 0.0)
        first, second = piece[:, :, :HALF], piece[:, :, HALF:]
        here = lane >= col_offset
        third_block = jnp.minimum(block + 2, grad.shape[3] // HALF - 1)
        for where_to, value in (
            (block, jnp.where(here, first, 0.0)),
            (block + 1, second),
            (third_block, jnp.where(here, 0.0, first)),
        ):
            cols = pl.ds(pl.multiple_of(where_to * HALF, HALF), HALF)
            grad[0, :, :, cols] = grad[0, :, :, cols] + value
        return carry

    lax.fori_loop(0, 4 * (RIM + 1), add, 0)


def deposit_call(idx_all, pieces, probe_sum, columns):
    vmem_spec = pl.BlockSpec(memory_space=pltpu.VMEM)
    return pl.pallas_call(
        deposit_kernel,
        out_shape=(
            jax.ShapeDtypeStruct((1, 2, STRIP, columns), F32),
            jax.ShapeDtypeStruct(probe_sum.shape, F32),
        ),
        in_specs=[pl.BlockSpec(memory_space=pltpu.SMEM), vmem_spec, vmem_spec],
        out_specs=(vmem_spec, vmem_spec),
        compiler_params=pltpu.CompilerParams(vmem_limit_bytes=32 * 1024 * 1024),
        name="deposit",
    )(idx_all, pieces, probe_sum)


def local(transmission, probe, exit_adjoint, scan_row, scan_col):
    head = jnp.concatenate([scan_row.reshape(1, 4), scan_col.reshape(1, 4)], axis=1)
    idx = jnp.pad(head, ((0, 7), (0, 120)))
    pieces, idx_all, probe_sum = main_call(transmission, probe, exit_adjoint, idx)
    object_grad, probe_grad = deposit_call(idx_all, pieces, probe_sum, transmission.shape[3])
    return object_grad, probe_grad.reshape(2, STRIP, SIDE)


def solution(mesh):
    placed = (
        P("depth", None, "scan", None),
        P(),
        P(None, "scan", None, None, None),
        P(None, "scan"),
        P(None, "scan"),
    )
    return jax.shard_map(
        local,
        mesh=mesh,
        in_specs=placed,
        out_specs=(P("depth", None, "scan", None), P(None, "depth", None)),
        check_vma=False,
    )
```

```python
import functools
import math

import jax
import jax.numpy as jnp
import numpy as np
from jax import lax
from jax.experimental import pallas as pl
from jax.experimental.pallas import tpu as pltpu
from jax.sharding import PartitionSpec as P

FRESNEL = 0.25
SIDE = 256
HALF = SIDE // 2
STRIP = 64
RIM = SIDE // STRIP
BATCHES = 2
PER = 2
F32 = jnp.float32
BF16 = jnp.bfloat16
MESH = pl.DeviceIdType.MESH


def tables():
    k = np.arange(SIDE)
    f = np.where(k < HALF, k, k - SIDE).astype(np.float64)
    h = np.exp(-1j * math.pi * FRESNEL * f * f / SIDE)
    dft = np.exp(-2j * math.pi * (np.outer(k, k) % SIDE) / SIDE)
    a = (dft.conj() / SIDE) @ (h[:, None] * dft)
    lefts, rights = [], []
    for sign in (1.0, -1.0):
        m = (a[:HALF, :HALF] + sign * a[:HALF, HALF:]) / 2.0
        left = np.block([[m.real, -m.imag], [m.imag, m.real]]).astype(np.float32)
        for out, full in ((lefts, left), (rights, left.T.copy())):
            high = full.astype(jnp.bfloat16)
            low = (full - high.astype(np.float32)).astype(jnp.bfloat16)
            out.append(np.stack([high, low]))
    return np.stack([np.stack(lefts), np.stack(rights)])


def dot(a, b):
    return jnp.dot(a, b, preferred_element_type=F32)


def split(x):
    high = x.astype(BF16)
    return high, (x - high.astype(F32)).astype(BF16)


def propagate(x_ref, w_ref, tab):
    middle = []
    for a in range(2):
        parts = []
        for ri in range(2):
            top, low = x_ref[ri, :HALF, :], x_ref[ri, HALF:, :]
            v = top + low if a == 0 else top - low
            l, r = v[:, :HALF], v[:, HALF:]
            parts.append(jnp.concatenate([l + r, l - r], axis=1))
        high, low = split(jnp.concatenate(parts, axis=0))
        left_high, left_low = tab[0, a, 0], tab[0, a, 1]
        middle.append(dot(left_high, high) + dot(left_low, high) + dot(left_high, low))
    sectors = []
    for b in range(2):
        cols = slice(b * HALF, (b + 1) * HALF)
        rows = [jnp.concatenate([z[:HALF, cols], z[HALF:, cols]], axis=1) for z in middle]
        high, low = split(jnp.concatenate(rows, axis=0))
        right_high, right_low = tab[1, b, 0], tab[1, b, 1]
        sectors.append(dot(high, right_high) + dot(high, right_low) + dot(low, right_high))
    for ri in range(2):
        cols = slice(ri * HALF, (ri + 1) * HALF)
        for half_col in range(2):
            s, d = sectors[0][:, cols], sectors[1][:, cols]
            v = s + d if half_col == 0 else s - d
            out = slice(half_col * HALF, (half_col + 1) * HALF)
            w_ref[ri, :HALF, out] = v[:HALF] + v[HALF:]
            w_ref[ri, HALF:, out] = v[:HALF] - v[HALF:]


def times(ar, ai, br, bi):
    return ar * br - ai * bi, ar * bi + ai * br


def main_kernel(
    across, hi_count, n_scan,
    trans, probe, exit_adjoint, table_in, idx_in,
    pieces, idx_all, probe_out,
    strip, tab, probe_v, exit_v, idx_s,
    sbuf, tbuf, x_v, start_v, w1_v, w2_v, w3_v, w4_v, zsend, zrecv,
    t_transit, g_transit, gbuf, total_v, part_s, part_r, rs_s, rs_r, ar_s, ar_r,
    local_sems, strip_sems, idx_send, idx_recv, t_send, t_recv, tt_send, tt_recv, z_send, z_recv,
    g_send, g_recv, gt_send, gt_recv, p_send, p_recv, rs_send, rs_recv, ar_send, ar_recv, ag_send, ag_recv,
):
    q = lax.axis_index("depth")
    j = lax.axis_index("scan")
    z = q // 2
    c = q % 2
    group = RIM * across
    member = j % group
    level = j // group
    y = j % RIM
    x = member // RIM
    span = RIM * (across - 1)

    def at(depth, scan):
        return {"depth": depth, "scan": scan}

    def region(step):
        return lax.rem(j + step + n_scan, n_scan)

    def mate(i):
        return level * group + lax.rem(member + i, group)

    def tier(i):
        return lax.rem(level + i, hi_count) * group + member

    loads = [
        pltpu.make_async_copy(table_in, tab, local_sems.at[1]),
        pltpu.make_async_copy(probe, probe_v, local_sems.at[2]),
        pltpu.make_async_copy(exit_adjoint.at[c], exit_v, local_sems.at[3]),
        pltpu.make_async_copy(idx_in, idx_all.at[0], local_sems.at[4]),
    ]

    def strip_copy(i):
        cols = pl.ds(pl.multiple_of(i * HALF, HALF), HALF)
        return pltpu.make_async_copy(trans.at[0, :, :, cols], strip.at[i], strip_sems.at[i])

    for copy in loads:
        copy.start()

    def start_strip(i, carry):
        strip_copy(i).start()
        return carry

    def wait_strip(i, carry):
        strip_copy(i).wait()
        return carry

    lax.fori_loop(0, strip.shape[0], start_strip, 0)

    barrier = pltpu.get_barrier_semaphore()
    partners = [at(q + 1 - 2 * c, j), at(q + 2 - 4 * z, j), at(3 - q, j)]
    for d in range(1, RIM + 1):
        for b in range(2):
            partners.append(at(2 * z + b, region(d)))
            partners.append(at(2 * z + b, region(-d)))
    for i in range(1, group):
        partners.append(at(q, mate(i)))
    for i in range(1, hi_count):
        partners.append(at(q, tier(i)))
    for device in partners:
        pl.semaphore_signal(barrier, inc=1, device_id=device, device_id_type=MESH)
    crossing = ((x == 0, span), (x == across - 1, -span))
    for edge, step in crossing:
        @pl.when(edge)
        def _(step=step):
            pl.semaphore_signal(
                barrier, inc=1, device_id=at(q + 1 - 2 * c, region(step)), device_id_type=MESH)
    on_edge = ((x == 0) | (x == across - 1)).astype(jnp.int32)
    pl.semaphore_wait(barrier, len(partners) + on_edge)

    idx_copies = [
        pltpu.make_async_remote_copy(
            src_ref=idx_in, dst_ref=idx_all.at[d], send_sem=idx_send.at[d], recv_sem=idx_recv.at[d],
            device_id=at(q, region(d)), device_id_type=MESH)
        for d in range(1, RIM + 1)
    ]
    for copy in idx_copies:
        copy.start()
    loads[3].wait()
    for copy in idx_copies:
        copy.wait_recv()
    to_smem = pltpu.make_async_copy(idx_all, idx_s, local_sems.at[5])
    to_smem.start()
    to_smem.wait()
    lax.fori_loop(0, strip.shape[0], wait_strip, 0)

    lane = lax.broadcasted_iota(jnp.int32, (1, 1, HALF), 2)
    last_block = strip.shape[0] - 1

    def t_copy(k, d, b, target, buffer=None):
        return pltpu.make_async_remote_copy(
            src_ref=sbuf.at[k, d, b], dst_ref=tbuf.at[k, c, d] if buffer is None else buffer,
            send_sem=t_send.at[k, d, b],
            recv_sem=t_recv.at[k, c, d] if buffer is None else tt_recv.at[k, d - 1 + c * (d // RIM)],
            device_id=at(2 * z + b, target), device_id_type=MESH)

    def t_start(k, d, b):
        if d == RIM:
            @pl.when(x == 0)
            def _():
                t_copy(k, d, b, region(span), t_transit.at[k, d - 1 + c]).start()

            @pl.when(x > 0)
            def _():
                t_copy(k, d, b, region(-d)).start()
            return

        turned = (y < d) & (c == b)

        @pl.when(turned)
        def _():
            t_copy(k, d, b, region(RIM - d), t_transit.at[k, d - 1]).start()

        @pl.when(jnp.logical_not(turned))
        def _():
            t_copy(k, d, b, region(-d)).start()

    def t_onward(k, slot, d, entry, step):
        return pltpu.make_async_remote_copy(
            src_ref=t_transit.at[k, entry], dst_ref=tbuf.at[k, slot, d],
            send_sem=tt_send.at[k, entry], recv_sem=t_recv.at[k, slot, d],
            device_id=at(q, region(step)), device_id_type=MESH)

    def t_transit_arrival(k, entry):
        return pltpu.make_async_remote_copy(
            src_ref=sbuf.at[k, 0, 0], dst_ref=t_transit.at[k, entry],
            send_sem=tt_send.at[k, entry], recv_sem=tt_recv.at[k, entry],
            device_id=at(q + 1 - 2 * c, j), device_id_type=MESH)

    def t_forward(k, act):
        @pl.when(x == across - 1)
        def _():
            for slot in range(2):
                act(t_transit_arrival(k, RIM - 1 + slot), t_onward(k, slot, RIM, RIM - 1 + slot, -RIM * across))

        for d in range(1, RIM):
            @pl.when(y >= RIM - d)
            def _(d=d):
                act(t_transit_arrival(k, d - 1), t_onward(k, c, d, d - 1, -RIM))

    def t_sibling(k):
        return pltpu.make_async_remote_copy(
            src_ref=sbuf.at[k, 0, 1 - c], dst_ref=tbuf.at[k, c, 0],
            send_sem=t_send.at[k, 0, 1], recv_sem=t_recv.at[k, c, 0],
            device_id=at(q + 1 - 2 * c, j), device_id_type=MESH)

    def t_local(k):
        return pltpu.make_async_copy(sbuf.at[k, 0, c], tbuf.at[k, c, 0], t_send.at[k, 0, 0])

    def t_arrival(k, slot, d):
        return pltpu.make_async_remote_copy(
            src_ref=sbuf.at[k, d, 0], dst_ref=tbuf.at[k, slot, d],
            send_sem=t_send.at[k, d, 0], recv_sem=t_recv.at[k, slot, d],
            device_id=at(q + 1 - 2 * c, j), device_id_type=MESH)

    def send_windows(k, carry):
        for d in (4, 3, 2, 1, 0):
            for b in range(2):
                col = idx_s[d, 2 + b, k]
                block = lax.shift_right_logical(col, 7)
                offset = col & (HALF - 1)
                first, second = strip[block], strip[block + 1]
                third = strip[jnp.minimum(block + 2, last_block)]
                sbuf[k, d, b, :, :, :HALF] = jnp.where(lane >= offset, first, third).astype(BF16)
                sbuf[k, d, b, :, :, HALF:] = second.astype(BF16)
                if d > 0:
                    t_start(k, d, b)
        t_sibling(k).start()
        t_local(k).start()
        return carry

    lax.fori_loop(0, PER, send_windows, 0)

    def wait_windows(k):
        for d in (0, 1, 2, 3, 4):
            if d == 0:
                t_local(k).wait()
                t_arrival(k, 1 - c, 0).wait_recv()
            else:
                for slot in range(2):
                    t_arrival(k, slot, d).wait_recv()

    row = lax.broadcasted_iota(jnp.int32, (STRIP, 1), 0)

    def offsets(k):
        return idx_s[0, c, k] & (STRIP - 1), idx_s[0, 2 + c, k] & (HALF - 1)

    def window(k, slot, block, row_offset):
        if block > 0:
            return tbuf[k, slot, block, 0].astype(F32), tbuf[k, slot, block, 1].astype(F32)
        here = row >= row_offset
        return tuple(
            jnp.where(here, tbuf[k, slot, 0, ri].astype(F32), tbuf[k, slot, RIM, ri].astype(F32))
            for ri in range(2)
        )

    blocks = [slice(i * STRIP, (i + 1) * STRIP) for i in range(RIM)]

    def roll(x, rows, cols):
        return pltpu.roll(pltpu.roll(x, rows, 0), cols, 1)

    def z_copy(k):
        return pltpu.make_async_remote_copy(
            src_ref=zsend.at[k], dst_ref=zrecv.at[k], send_sem=z_send.at[k], recv_sem=z_recv.at[k],
            device_id=at(q + 2 - 4 * z, j), device_id_type=MESH)

    for copy in loads[:3]:
        copy.wait()

    def first_half(k, carry):
        row_offset, col_offset = offsets(k)

        @pl.when(z == 0)
        def _():
            for ri in range(2):
                start_v[k, ri] = roll(probe_v[ri], row_offset, col_offset)
            wait_windows(k)
            for i, rows in enumerate(blocks):
                tr, ti = window(k, 0, i, row_offset)
                x_v[0, rows, :], x_v[1, rows, :] = times(tr, ti, start_v[k, 0, rows, :], start_v[k, 1, rows, :])

        @pl.when(z == 1)
        def _():
            x_v[0] = roll(exit_v[k, 0], row_offset, col_offset)
            x_v[1] = -roll(exit_v[k, 1], row_offset, col_offset)

        propagate(x_v, w1_v.at[k], tab)

        @pl.when(z == 1)
        def _():
            wait_windows(k)

        for i, rows in enumerate(blocks):
            tr, ti = window(k, 1, i, row_offset)
            x_v[0, rows, :], x_v[1, rows, :] = times(tr, ti, w1_v[k, 0, rows, :], w1_v[k, 1, rows, :])
        propagate(x_v, w2_v.at[k], tab)

        @pl.when(z == 0)
        def _():
            zsend[k] = w2_v[k].astype(BF16)

        @pl.when(z == 1)
        def _():
            for i, rows in enumerate(blocks):
                tr, ti = window(k, 0, i, row_offset)
                vr, vi = times(tr, ti, w2_v[k, 0, rows, :], w2_v[k, 1, rows, :])
                zsend[k, 0, rows, :] = vr.astype(BF16)
                zsend[k, 1, rows, :] = vi.astype(BF16)

        z_copy(k).start()
        return carry

    def forward_windows(k):
        def act(arrival, onward):
            arrival.wait_recv()
            onward.start()
        t_forward(k, act)

    def windows_and_first_half(k, carry):
        forward_windows(k)
        return first_half(k, carry)

    lax.fori_loop(0, PER, windows_and_first_half, 0)

    def g_copy(k, slot, d, target, buffer=None):
        return pltpu.make_async_remote_copy(
            src_ref=gbuf.at[k, slot, d % RIM], dst_ref=pieces.at[k, c, d] if buffer is None else buffer,
            send_sem=g_send.at[k, slot, d],
            recv_sem=g_recv.at[k, c, d] if buffer is None else gt_recv.at[k, d - 1 + c * (d // RIM)],
            device_id=at(2 * z + slot, target), device_id_type=MESH)

    def g_start(k, slot, d):
        if d == RIM:
            @pl.when(x == across - 1)
            def _():
                g_copy(k, slot, d, region(-span), g_transit.at[k, d - 1 + c]).start()

            @pl.when(x < across - 1)
            def _():
                g_copy(k, slot, d, region(d)).start()
            return

        turned = (y + d >= RIM) & (c == slot)

        @pl.when(turned)
        def _():
            g_copy(k, slot, d, region(d - RIM), g_transit.at[k, d - 1]).start()

        @pl.when(jnp.logical_not(turned))
        def _():
            g_copy(k, slot, d, region(d)).start()

    def g_onward(k, core, d, entry, step):
        return pltpu.make_async_remote_copy(
            src_ref=g_transit.at[k, entry], dst_ref=pieces.at[k, core, d],
            send_sem=gt_send.at[k, entry], recv_sem=g_recv.at[k, core, d],
            device_id=at(q, region(step)), device_id_type=MESH)

    def g_transit_arrival(k, entry):
        return pltpu.make_async_remote_copy(
            src_ref=gbuf.at[k, 0, 0], dst_ref=g_transit.at[k, entry],
            send_sem=gt_send.at[k, entry], recv_sem=gt_recv.at[k, entry],
            device_id=at(q + 1 - 2 * c, j), device_id_type=MESH)

    def g_forward(k, act):
        @pl.when(x == 0)
        def _():
            for core in range(2):
                act(g_transit_arrival(k, RIM - 1 + core), g_onward(k, core, RIM, RIM - 1 + core, RIM * across))

        for d in range(1, RIM):
            @pl.when(y < d)
            def _(d=d):
                act(g_transit_arrival(k, d - 1), g_onward(k, c, d, d - 1, RIM))

    def forward_pieces(k):
        def act(arrival, onward):
            arrival.wait_recv()
            onward.start()
        g_forward(k, act)

    def g_sibling(k):
        return pltpu.make_async_remote_copy(
            src_ref=gbuf.at[k, 1 - c, 0], dst_ref=pieces.at[k, c, 0],
            send_sem=g_send.at[k, 1, 0], recv_sem=g_recv.at[k, c, 0],
            device_id=at(q + 1 - 2 * c, j), device_id_type=MESH)

    def g_local(k):
        return pltpu.make_async_copy(gbuf.at[k, c, 0], pieces.at[k, c, 0], g_send.at[k, 0, 0])

    def g_arrival(k, core, d):
        return pltpu.make_async_remote_copy(
            src_ref=gbuf.at[k, 0, d % RIM], dst_ref=pieces.at[k, core, d],
            send_sem=g_send.at[k, 0, d], recv_sem=g_recv.at[k, core, d],
            device_id=at(q + 1 - 2 * c, j), device_id_type=MESH)

    def second_half(k, carry):
        row_offset, col_offset = offsets(k)
        z_copy(k).wait_recv()

        @pl.when(z == 0)
        def _():
            x_v[...] = zrecv[k].astype(F32)

        @pl.when(z == 1)
        def _():
            for i, rows in enumerate(blocks):
                tr, ti = window(k, 0, i, row_offset)
                vr, vi = zrecv[k, 0, rows, :].astype(F32), zrecv[k, 1, rows, :].astype(F32)
                x_v[0, rows, :], x_v[1, rows, :] = times(tr, ti, vr, vi)
                gr, gi = times(vr, vi, w2_v[k, 0, rows, :], w2_v[k, 1, rows, :])
                gbuf[k, 0, i, 0] = gr.astype(BF16)
                gbuf[k, 0, i, 1] = (-gi).astype(BF16)

        propagate(x_v, w3_v, tab)
        for i, rows in enumerate(blocks):
            gr, gi = times(w1_v[k, 0, rows, :], w1_v[k, 1, rows, :], w3_v[0, rows, :], w3_v[1, rows, :])
            gbuf[k, 1, i, 0] = gr.astype(BF16)
            gbuf[k, 1, i, 1] = (-gi).astype(BF16)
        for d in (4, 3, 2, 1):
            g_start(k, 1, d)

        @pl.when(z == 0)
        def _():
            for i, rows in enumerate(blocks):
                tr, ti = window(k, 1, i, row_offset)
                x_v[0, rows, :], x_v[1, rows, :] = times(tr, ti, w3_v[0, rows, :], w3_v[1, rows, :])
            propagate(x_v, w4_v, tab)
            for i, rows in enumerate(blocks):
                wr, wi = w4_v[0, rows, :], w4_v[1, rows, :]
                gr, gi = times(start_v[k, 0, rows, :], start_v[k, 1, rows, :], wr, wi)
                gbuf[k, 0, i, 0] = gr.astype(BF16)
                gbuf[k, 0, i, 1] = (-gi).astype(BF16)

        for d in (4, 3, 2, 1):
            g_start(k, 0, d)
        g_sibling(k).start()
        g_local(k).start()

        @pl.when(z == 0)
        def _():
            for i, rows in enumerate(blocks):
                tr, ti = window(k, 0, i, row_offset)
                vr, vi = times(tr, ti, w4_v[0, rows, :], w4_v[1, rows, :])
                x_v[0, rows, :], x_v[1, rows, :] = vr, -vi
            back_rows, back_cols = (SIDE - row_offset) & (SIDE - 1), (SIDE - col_offset) & (SIDE - 1)
            for ri in range(2):
                moved = roll(x_v[ri], back_rows, back_cols)
                total_v[ri] = jnp.where(k > 0, total_v[ri], 0.0) + moved

        return carry

    lax.fori_loop(0, PER, second_half, 0)

    def p_copy(section):
        return pltpu.make_async_remote_copy(
            src_ref=part_s.at[section], dst_ref=part_r.at[c], send_sem=p_send.at[section],
            recv_sem=p_recv.at[c], device_id=at(section, j), device_id_type=MESH)

    def p_arrival(core):
        return pltpu.make_async_remote_copy(
            src_ref=part_s.at[0], dst_ref=part_r.at[core], send_sem=p_send.at[0],
            recv_sem=p_recv.at[core], device_id=at(q + 1 - 2 * c, j), device_id_type=MESH)

    @pl.when(z == 0)
    def _():
        for section in range(4):
            part_s[section] = total_v[:, section * STRIP:(section + 1) * STRIP, :].astype(BF16)
        p_copy(2).start()
        p_copy(3).start()
        p_copy(1 - c).start()

    forward_pieces(0)
    forward_pieces(1)

    @pl.when(z == 0)
    def _():
        own = pltpu.make_async_copy(part_s.at[c], part_r.at[c], p_send.at[c])
        own.start()
        own.wait()
        p_arrival(1 - c).wait_recv()

    @pl.when(z == 1)
    def _():
        p_arrival(0).wait_recv()
        p_arrival(1).wait_recv()

    block_sum = part_r[0].astype(F32) + part_r[1].astype(F32)
    rs_s[...] = block_sum.reshape(rs_s.shape)

    def rs_copy(i):
        target = lax.rem(member + i, group)
        return pltpu.make_async_remote_copy(
            src_ref=rs_s.at[target], dst_ref=rs_r.at[member], send_sem=rs_send.at[i],
            recv_sem=rs_recv.at[i], device_id=at(q, mate(i)), device_id_type=MESH)

    for i in range(1, group):
        rs_copy(i).start()
    rs_r[member] = rs_s[member]
    for i in range(1, group):
        rs_copy(i).wait_recv()
    piece_sum = rs_r[0]
    for m in range(1, group):
        piece_sum = piece_sum + rs_r[m]
    ar_s[...] = piece_sum
    ar_r[level] = piece_sum

    def ar_copy(i):
        return pltpu.make_async_remote_copy(
            src_ref=ar_s, dst_ref=ar_r.at[level], send_sem=ar_send.at[i],
            recv_sem=ar_recv.at[i], device_id=at(q, tier(i)), device_id_type=MESH)

    for i in range(1, hi_count):
        ar_copy(i).start()
    for i in range(1, hi_count):
        ar_copy(i).wait()
    piece_sum = ar_r[0]
    for m in range(1, hi_count):
        piece_sum = piece_sum + ar_r[m]
    probe_out[member] = piece_sum

    def ag_copy(i):
        return pltpu.make_async_remote_copy(
            src_ref=probe_out.at[member], dst_ref=probe_out.at[member], send_sem=ag_send.at[i],
            recv_sem=ag_recv.at[i], device_id=at(q, mate(i)), device_id_type=MESH)

    for i in range(1, group):
        ag_copy(i).start()
    for i in range(1, group):
        ag_copy(i).wait()

    for copy in idx_copies:
        copy.wait_send()
    for i in range(1, group):
        rs_copy(i).wait_send()

    @pl.when(z == 0)
    def _():
        p_copy(2).wait_send()
        p_copy(3).wait_send()
        p_copy(1 - c).wait_send()

    def drain(k, carry):
        z_copy(k).wait_send()
        t_sibling(k).wait_send()
        g_sibling(k).wait_send()
        g_local(k).wait()
        g_arrival(k, 1 - c, 0).wait_recv()

        def act(arrival, onward):
            onward.wait_send()

        t_forward(k, act)
        g_forward(k, act)
        for d in range(1, RIM + 1):
            for b in range(2):
                t_copy(k, d, b, region(-d)).wait_send()
                g_copy(k, b, d, region(d)).wait_send()
                g_arrival(k, b, d).wait_recv()
        return carry

    lax.fori_loop(0, PER, drain, 0)


def main_call(transmission, probe, exit_adjoint, idx):
    n_scan = lax.axis_size("scan")
    across = 4 if n_scan == 64 else 2
    group = RIM * across
    hi_count = n_scan // group
    piece = (16 // group, 8, SIDE)
    hbm_spec = pl.BlockSpec(memory_space=pltpu.HBM)
    vmem_spec = pl.BlockSpec(memory_space=pltpu.VMEM)
    field = (2, SIDE, SIDE)
    dma = pltpu.SemaphoreType.DMA
    columns = transmission.shape[3]
    return pl.pallas_call(
        functools.partial(main_kernel, across, hi_count, n_scan),
        out_shape=(
            jax.ShapeDtypeStruct((PER, 2, RIM + 1, 2, STRIP, SIDE), BF16),
            jax.ShapeDtypeStruct((RIM + 1, 8, 128), jnp.int32),
            jax.ShapeDtypeStruct((group,) + piece, F32),
        ),
        in_specs=[hbm_spec] * 5,
        out_specs=(hbm_spec, hbm_spec, vmem_spec),
        scratch_shapes=[
            pltpu.VMEM((columns // HALF, 2, STRIP, HALF), F32),
            pltpu.VMEM((2, 2, 2, SIDE, SIDE), BF16),
            pltpu.VMEM(field, F32),
            pltpu.VMEM((PER,) + field, F32),
            pltpu.SMEM((RIM + 1, 8, 128), jnp.int32),
            pltpu.VMEM((PER, RIM + 1, 2, 2, STRIP, SIDE), BF16),
            pltpu.VMEM((PER, 2, RIM + 1, 2, STRIP, SIDE), BF16),
            pltpu.VMEM(field, F32),
            pltpu.VMEM((PER,) + field, F32),
            pltpu.VMEM((PER,) + field, F32),
            pltpu.VMEM((PER,) + field, F32),
            pltpu.VMEM(field, F32),
            pltpu.VMEM(field, F32),
            pltpu.VMEM((PER,) + field, BF16),
            pltpu.VMEM((PER,) + field, BF16),
            pltpu.VMEM((PER, RIM + 1, 2, STRIP, SIDE), BF16),
            pltpu.VMEM((PER, RIM + 1, 2, STRIP, SIDE), BF16),
            pltpu.VMEM((PER, 2, RIM, 2, STRIP, SIDE), BF16),
            pltpu.VMEM(field, F32),
            pltpu.VMEM((4, 2, STRIP, SIDE), BF16),
            pltpu.VMEM((2, 2, STRIP, SIDE), BF16),
            pltpu.VMEM((group,) + piece, F32),
            pltpu.VMEM((group,) + piece, F32),
            pltpu.VMEM(piece, F32),
            pltpu.VMEM((hi_count,) + piece, F32),
            dma((6,)),
            dma((columns // HALF,)),
            dma((RIM + 1,)),
            dma((RIM + 1,)),
            dma((PER, RIM + 1, 2)),
            dma((PER, 2, RIM + 1)),
            dma((PER, RIM + 1)),
            dma((PER, RIM + 1)),
            dma((PER,)),
            dma((PER,)),
            dma((PER, 2, RIM + 1)),
            dma((PER, 2, RIM + 1)),
            dma((PER, RIM + 1)),
            dma((PER, RIM + 1)),
            dma((4,)),
            dma((2,)),
            dma((group,)),
            dma((group,)),
            dma((hi_count,)),
            dma((hi_count,)),
            dma((group,)),
            dma((group,)),
        ],
        compiler_params=pltpu.CompilerParams(
            collective_id=0, has_side_effects=True, vmem_limit_bytes=48 * 1024 * 1024
        ),
        cost_estimate=pl.CostEstimate(flops=8 * 12 * 2 * SIDE**3, bytes_accessed=8 << 20, transcendentals=0),
        name="waves",
    )(transmission, probe, exit_adjoint, jnp.asarray(tables()), idx)


def deposit_kernel(idx, pieces, probe_in, grad, probe_out):
    probe_out[...] = probe_in[...]
    grad[...] = jnp.zeros_like(grad)
    lane = lax.broadcasted_iota(jnp.int32, (1, 1, HALF), 2)
    row = lax.broadcasted_iota(jnp.int32, (1, STRIP, 1), 1)

    def add(n, carry):
        d = n // 4
        core = (n // 2) % 2
        k = n % 2
        row_offset = idx[d, core, k] & (STRIP - 1)
        col = idx[d, 2 + core, k]
        block = lax.shift_right_logical(col, 7)
        col_offset = col & (HALF - 1)
        low = jnp.where(d == 0, row_offset, 0)
        high = jnp.where(d == RIM, row_offset, STRIP)
        keep = (row >= low) & (row < high)
        piece = jnp.where(keep, pieces[k, core, d].astype(F32), 0.0)
        first, second = piece[:, :, :HALF], piece[:, :, HALF:]
        here = lane >= col_offset
        third_block = jnp.minimum(block + 2, grad.shape[3] // HALF - 1)
        for where_to, value in (
            (block, jnp.where(here, first, 0.0)),
            (block + 1, second),
            (third_block, jnp.where(here, 0.0, first)),
        ):
            cols = pl.ds(pl.multiple_of(where_to * HALF, HALF), HALF)
            grad[0, :, :, cols] = grad[0, :, :, cols] + value
        return carry

    lax.fori_loop(0, 4 * (RIM + 1), add, 0)


def deposit_call(idx_all, pieces, probe_sum, columns):
    vmem_spec = pl.BlockSpec(memory_space=pltpu.VMEM)
    return pl.pallas_call(
        deposit_kernel,
        out_shape=(
            jax.ShapeDtypeStruct((1, 2, STRIP, columns), F32),
            jax.ShapeDtypeStruct(probe_sum.shape, F32),
        ),
        in_specs=[pl.BlockSpec(memory_space=pltpu.SMEM), vmem_spec, vmem_spec],
        out_specs=(vmem_spec, vmem_spec),
        compiler_params=pltpu.CompilerParams(vmem_limit_bytes=32 * 1024 * 1024),
        name="deposit",
    )(idx_all, pieces, probe_sum)


def local(transmission, probe, exit_adjoint, scan_row, scan_col):
    idx = jnp.pad(jnp.concatenate([scan_row, scan_col], axis=0), ((0, 4), (0, 126)))
    pieces, idx_all, probe_sum = main_call(transmission, probe, exit_adjoint, idx)
    object_grad, probe_grad = deposit_call(idx_all, pieces, probe_sum, transmission.shape[3])
    return object_grad, probe_grad.reshape(2, STRIP, SIDE)


def solution(mesh):
    placed = (
        P("depth", None, "scan", None),
        P(),
        P(None, "scan", None, None, None),
        P(None, "scan"),
        P(None, "scan"),
    )
    return jax.shard_map(
        local,
        mesh=mesh,
        in_specs=placed,
        out_specs=(P("depth", None, "scan", None), P(None, "depth", None)),
        check_vma=False,
    )
```

```python
import functools
import math

import jax
import jax.numpy as jnp
import numpy as np
from jax import lax
from jax.experimental import pallas as pl
from jax.experimental.pallas import tpu as pltpu
from jax.sharding import PartitionSpec as P

FRESNEL = 0.25
SIDE = 256
HALF = SIDE // 2
STRIP = 64
RIM = SIDE // STRIP
BATCHES = 2
PER = 2
F32 = jnp.float32
BF16 = jnp.bfloat16
MESH = pl.DeviceIdType.MESH


def tables():
    k = np.arange(SIDE)
    f = np.where(k < HALF, k, k - SIDE).astype(np.float64)
    h = np.exp(-1j * math.pi * FRESNEL * f * f / SIDE)
    dft = np.exp(-2j * math.pi * (np.outer(k, k) % SIDE) / SIDE)
    a = (dft.conj() / SIDE) @ (h[:, None] * dft)
    lefts, rights = [], []
    for sign in (1.0, -1.0):
        m = (a[:HALF, :HALF] + sign * a[:HALF, HALF:]) / 2.0
        left = np.block([[m.real, -m.imag], [m.imag, m.real]]).astype(np.float32)
        for out, full in ((lefts, left), (rights, left.T.copy())):
            high = full.astype(jnp.bfloat16)
            low = (full - high.astype(np.float32)).astype(jnp.bfloat16)
            out.append(np.stack([high, low]))
    return np.stack([np.stack(lefts), np.stack(rights)])


def dot(a, b):
    return jnp.dot(a, b, preferred_element_type=F32)


def split(x):
    high = x.astype(BF16)
    return high, (x - high.astype(F32)).astype(BF16)


def propagate(x_ref, w_ref, tab):
    middle = []
    for a in range(2):
        parts = []
        for ri in range(2):
            top, low = x_ref[ri, :HALF, :], x_ref[ri, HALF:, :]
            v = top + low if a == 0 else top - low
            l, r = v[:, :HALF], v[:, HALF:]
            parts.append(jnp.concatenate([l + r, l - r], axis=1))
        high, low = split(jnp.concatenate(parts, axis=0))
        left_high, left_low = tab[0, a, 0], tab[0, a, 1]
        middle.append(dot(left_high, high) + dot(left_low, high) + dot(left_high, low))
    sectors = []
    for b in range(2):
        cols = slice(b * HALF, (b + 1) * HALF)
        rows = [jnp.concatenate([z[:HALF, cols], z[HALF:, cols]], axis=1) for z in middle]
        high, low = split(jnp.concatenate(rows, axis=0))
        right_high, right_low = tab[1, b, 0], tab[1, b, 1]
        sectors.append(dot(high, right_high) + dot(high, right_low) + dot(low, right_high))
    for ri in range(2):
        cols = slice(ri * HALF, (ri + 1) * HALF)
        for half_col in range(2):
            s, d = sectors[0][:, cols], sectors[1][:, cols]
            v = s + d if half_col == 0 else s - d
            out = slice(half_col * HALF, (half_col + 1) * HALF)
            w_ref[ri, :HALF, out] = v[:HALF] + v[HALF:]
            w_ref[ri, HALF:, out] = v[:HALF] - v[HALF:]


def times(ar, ai, br, bi):
    return ar * br - ai * bi, ar * bi + ai * br


def main_kernel(
    across, hi_count, n_scan,
    trans, probe, exit_adjoint, table_in, idx_in,
    pieces, idx_all, probe_out,
    strip, tab, probe_v, exit_v, idx_s,
    sbuf, tbuf, x_v, start_v, w1_v, w2_v, w3_v, w4_v, zsend, zrecv,
    t_transit, g_transit, gbuf, total_v, part_r, rs_s, rs_r, ar_s, ar_r,
    local_sems, strip_sems, idx_send, idx_recv, t_send, t_recv, tt_send, tt_recv, z_send, z_recv,
    g_send, g_recv, gt_send, gt_recv, p_send, p_recv, rs_send, rs_recv, ar_send, ar_recv, ag_send, ag_recv,
):
    q = lax.axis_index("depth")
    j = lax.axis_index("scan")
    z = q // 2
    c = q % 2
    group = RIM * across
    member = j % group
    level = j // group
    y = j % RIM
    x = member // RIM
    span = RIM * (across - 1)

    def at(depth, scan):
        return {"depth": depth, "scan": scan}

    def region(step):
        return lax.rem(j + step + n_scan, n_scan)

    def mate(i):
        return level * group + lax.rem(member + i, group)

    def tier(i):
        return lax.rem(level + i, hi_count) * group + member

    loads = [
        pltpu.make_async_copy(table_in, tab, local_sems.at[1]),
        pltpu.make_async_copy(probe, probe_v, local_sems.at[2]),
        pltpu.make_async_copy(exit_adjoint.at[c], exit_v, local_sems.at[3]),
        pltpu.make_async_copy(idx_in, idx_all.at[0], local_sems.at[4]),
    ]

    def strip_copy(i):
        cols = pl.ds(pl.multiple_of(i * HALF, HALF), HALF)
        return pltpu.make_async_copy(trans.at[0, :, :, cols], strip.at[i], strip_sems.at[i])

    for copy in loads:
        copy.start()

    def start_strip(i, carry):
        strip_copy(i).start()
        return carry

    def wait_strip(i, carry):
        strip_copy(i).wait()
        return carry

    lax.fori_loop(0, strip.shape[0], start_strip, 0)

    barrier = pltpu.get_barrier_semaphore()
    partners = [at(q + 1 - 2 * c, j), at(q + 2 - 4 * z, j)]
    for d in range(1, RIM + 1):
        for b in range(2):
            partners.append(at(2 * z + b, region(d)))
            partners.append(at(2 * z + b, region(-d)))
    for i in range(1, group):
        partners.append(at(q, mate(i)))
    for i in range(1, hi_count):
        partners.append(at(q, tier(i)))
        partners.append(at(q + 2 - 4 * z, tier(i)))
    for device in partners:
        pl.semaphore_signal(barrier, inc=1, device_id=device, device_id_type=MESH)
    crossing = ((x == 0, span), (x == across - 1, -span))
    for edge, step in crossing:
        @pl.when(edge)
        def _(step=step):
            pl.semaphore_signal(
                barrier, inc=1, device_id=at(q + 1 - 2 * c, region(step)), device_id_type=MESH)
    on_edge = ((x == 0) | (x == across - 1)).astype(jnp.int32)
    pl.semaphore_wait(barrier, len(partners) + on_edge)

    idx_copies = [
        pltpu.make_async_remote_copy(
            src_ref=idx_in, dst_ref=idx_all.at[d], send_sem=idx_send.at[d], recv_sem=idx_recv.at[d],
            device_id=at(q, region(d)), device_id_type=MESH)
        for d in range(1, RIM + 1)
    ]
    for copy in idx_copies:
        copy.start()
    loads[3].wait()
    for copy in idx_copies:
        copy.wait_recv()
    to_smem = pltpu.make_async_copy(idx_all, idx_s, local_sems.at[5])
    to_smem.start()
    to_smem.wait()
    lax.fori_loop(0, strip.shape[0], wait_strip, 0)

    lane = lax.broadcasted_iota(jnp.int32, (1, 1, HALF), 2)
    last_block = strip.shape[0] - 1

    def t_copy(k, d, b, target, buffer=None):
        return pltpu.make_async_remote_copy(
            src_ref=sbuf.at[k, d, b], dst_ref=tbuf.at[k, c, d] if buffer is None else buffer,
            send_sem=t_send.at[k, d, b],
            recv_sem=t_recv.at[k, c, d] if buffer is None else tt_recv.at[k, d - 1 + c * (d // RIM)],
            device_id=at(2 * z + b, target), device_id_type=MESH)

    def t_start(k, d, b):
        if d == RIM:
            @pl.when(x == 0)
            def _():
                t_copy(k, d, b, region(span), t_transit.at[k, d - 1 + c]).start()

            @pl.when(x > 0)
            def _():
                t_copy(k, d, b, region(-d)).start()
            return

        turned = (y < d) & (c == b)

        @pl.when(turned)
        def _():
            t_copy(k, d, b, region(RIM - d), t_transit.at[k, d - 1]).start()

        @pl.when(jnp.logical_not(turned))
        def _():
            t_copy(k, d, b, region(-d)).start()

    def t_onward(k, slot, d, entry, step):
        return pltpu.make_async_remote_copy(
            src_ref=t_transit.at[k, entry], dst_ref=tbuf.at[k, slot, d],
            send_sem=tt_send.at[k, entry], recv_sem=t_recv.at[k, slot, d],
            device_id=at(q, region(step)), device_id_type=MESH)

    def t_transit_arrival(k, entry):
        return pltpu.make_async_remote_copy(
            src_ref=sbuf.at[k, 0, 0], dst_ref=t_transit.at[k, entry],
            send_sem=tt_send.at[k, entry], recv_sem=tt_recv.at[k, entry],
            device_id=at(q + 1 - 2 * c, j), device_id_type=MESH)

    def t_forward(k, act):
        @pl.when(x == across - 1)
        def _():
            for slot in range(2):
                act(t_transit_arrival(k, RIM - 1 + slot), t_onward(k, slot, RIM, RIM - 1 + slot, -RIM * across))

        for d in range(1, RIM):
            @pl.when(y >= RIM - d)
            def _(d=d):
                act(t_transit_arrival(k, d - 1), t_onward(k, c, d, d - 1, -RIM))

    def t_sibling(k):
        return pltpu.make_async_remote_copy(
            src_ref=sbuf.at[k, 0, 1 - c], dst_ref=tbuf.at[k, c, 0],
            send_sem=t_send.at[k, 0, 1], recv_sem=t_recv.at[k, c, 0],
            device_id=at(q + 1 - 2 * c, j), device_id_type=MESH)

    def t_local(k):
        return pltpu.make_async_copy(sbuf.at[k, 0, c], tbuf.at[k, c, 0], t_send.at[k, 0, 0])

    def t_arrival(k, slot, d):
        return pltpu.make_async_remote_copy(
            src_ref=sbuf.at[k, d, 0], dst_ref=tbuf.at[k, slot, d],
            send_sem=t_send.at[k, d, 0], recv_sem=t_recv.at[k, slot, d],
            device_id=at(q + 1 - 2 * c, j), device_id_type=MESH)

    def send_windows(k, carry):
        for d in (4, 3, 2, 1, 0):
            for b in range(2):
                col = idx_s[d, 2 + b, k]
                block = lax.shift_right_logical(col, 7)
                offset = col & (HALF - 1)
                first, second = strip[block], strip[block + 1]
                third = strip[jnp.minimum(block + 2, last_block)]
                sbuf[k, d, b, :, :, :HALF] = jnp.where(lane >= offset, first, third).astype(BF16)
                sbuf[k, d, b, :, :, HALF:] = second.astype(BF16)
                if d > 0:
                    t_start(k, d, b)
        t_sibling(k).start()
        t_local(k).start()
        return carry

    lax.fori_loop(0, PER, send_windows, 0)

    def wait_windows(k):
        for d in (0, 1, 2, 3, 4):
            if d == 0:
                t_local(k).wait()
                t_arrival(k, 1 - c, 0).wait_recv()
            else:
                for slot in range(2):
                    t_arrival(k, slot, d).wait_recv()

    row = lax.broadcasted_iota(jnp.int32, (STRIP, 1), 0)

    def offsets(k):
        return idx_s[0, c, k] & (STRIP - 1), idx_s[0, 2 + c, k] & (HALF - 1)

    def window(k, slot, block, row_offset):
        if block > 0:
            return tbuf[k, slot, block, 0].astype(F32), tbuf[k, slot, block, 1].astype(F32)
        here = row >= row_offset
        return tuple(
            jnp.where(here, tbuf[k, slot, 0, ri].astype(F32), tbuf[k, slot, RIM, ri].astype(F32))
            for ri in range(2)
        )

    blocks = [slice(i * STRIP, (i + 1) * STRIP) for i in range(RIM)]

    def roll(x, rows, cols):
        return pltpu.roll(pltpu.roll(x, rows, 0), cols, 1)

    def z_copy(k):
        return pltpu.make_async_remote_copy(
            src_ref=zsend.at[k], dst_ref=zrecv.at[k], send_sem=z_send.at[k], recv_sem=z_recv.at[k],
            device_id=at(q + 2 - 4 * z, j), device_id_type=MESH)

    for copy in loads[:3]:
        copy.wait()

    def first_half(k):
        row_offset, col_offset = offsets(k)

        @pl.when(z == 0)
        def _():
            for ri in range(2):
                start_v[k, ri] = roll(probe_v[ri], row_offset, col_offset)
            wait_windows(k)
            for i, rows in enumerate(blocks):
                tr, ti = window(k, 0, i, row_offset)
                x_v[0, rows, :], x_v[1, rows, :] = times(tr, ti, start_v[k, 0, rows, :], start_v[k, 1, rows, :])

        @pl.when(z == 1)
        def _():
            x_v[0] = roll(exit_v[k, 0], row_offset, col_offset)
            x_v[1] = -roll(exit_v[k, 1], row_offset, col_offset)

        propagate(x_v, w1_v.at[k], tab)

        @pl.when(z == 1)
        def _():
            wait_windows(k)

        for i, rows in enumerate(blocks):
            tr, ti = window(k, 1, i, row_offset)
            x_v[0, rows, :], x_v[1, rows, :] = times(tr, ti, w1_v[k, 0, rows, :], w1_v[k, 1, rows, :])
        propagate(x_v, w2_v.at[k], tab)

        @pl.when(z == 0)
        def _():
            zsend[k] = w2_v[k].astype(BF16)

        @pl.when(z == 1)
        def _():
            for i, rows in enumerate(blocks):
                tr, ti = window(k, 0, i, row_offset)
                vr, vi = times(tr, ti, w2_v[k, 0, rows, :], w2_v[k, 1, rows, :])
                zsend[k, 0, rows, :] = vr.astype(BF16)
                zsend[k, 1, rows, :] = vi.astype(BF16)

        z_copy(k).start()

    def forward_windows(k):
        def act(arrival, onward):
            arrival.wait_recv()
            onward.start()
        t_forward(k, act)


    def g_copy(k, slot, d, target, buffer=None):
        return pltpu.make_async_remote_copy(
            src_ref=gbuf.at[k, slot, d % RIM], dst_ref=pieces.at[k, c, d] if buffer is None else buffer,
            send_sem=g_send.at[k, slot, d],
            recv_sem=g_recv.at[k, c, d] if buffer is None else gt_recv.at[k, d - 1 + c * (d // RIM)],
            device_id=at(2 * z + slot, target), device_id_type=MESH)

    def g_start(k, slot, d):
        if d == RIM:
            @pl.when(x == across - 1)
            def _():
                g_copy(k, slot, d, region(-span), g_transit.at[k, d - 1 + c]).start()

            @pl.when(x < across - 1)
            def _():
                g_copy(k, slot, d, region(d)).start()
            return

        turned = (y + d >= RIM) & (c == slot)

        @pl.when(turned)
        def _():
            g_copy(k, slot, d, region(d - RIM), g_transit.at[k, d - 1]).start()

        @pl.when(jnp.logical_not(turned))
        def _():
            g_copy(k, slot, d, region(d)).start()

    def g_onward(k, core, d, entry, step):
        return pltpu.make_async_remote_copy(
            src_ref=g_transit.at[k, entry], dst_ref=pieces.at[k, core, d],
            send_sem=gt_send.at[k, entry], recv_sem=g_recv.at[k, core, d],
            device_id=at(q, region(step)), device_id_type=MESH)

    def g_transit_arrival(k, entry):
        return pltpu.make_async_remote_copy(
            src_ref=gbuf.at[k, 0, 0], dst_ref=g_transit.at[k, entry],
            send_sem=gt_send.at[k, entry], recv_sem=gt_recv.at[k, entry],
            device_id=at(q + 1 - 2 * c, j), device_id_type=MESH)

    def g_forward(k, act):
        @pl.when(x == 0)
        def _():
            for core in range(2):
                act(g_transit_arrival(k, RIM - 1 + core), g_onward(k, core, RIM, RIM - 1 + core, RIM * across))

        for d in range(1, RIM):
            @pl.when(y < d)
            def _(d=d):
                act(g_transit_arrival(k, d - 1), g_onward(k, c, d, d - 1, RIM))

    def forward_pieces(k):
        def act(arrival, onward):
            arrival.wait_recv()
            onward.start()
        g_forward(k, act)

    def g_sibling(k):
        return pltpu.make_async_remote_copy(
            src_ref=gbuf.at[k, 1 - c, 0], dst_ref=pieces.at[k, c, 0],
            send_sem=g_send.at[k, 1, 0], recv_sem=g_recv.at[k, c, 0],
            device_id=at(q + 1 - 2 * c, j), device_id_type=MESH)

    def g_local(k):
        return pltpu.make_async_copy(gbuf.at[k, c, 0], pieces.at[k, c, 0], g_send.at[k, 0, 0])

    def g_arrival(k, core, d):
        return pltpu.make_async_remote_copy(
            src_ref=gbuf.at[k, 0, d % RIM], dst_ref=pieces.at[k, core, d],
            send_sem=g_send.at[k, 0, d], recv_sem=g_recv.at[k, core, d],
            device_id=at(q + 1 - 2 * c, j), device_id_type=MESH)

    def second_half(k):
        row_offset, col_offset = offsets(k)
        z_copy(k).wait_recv()

        @pl.when(z == 0)
        def _():
            x_v[...] = zrecv[k].astype(F32)

        @pl.when(z == 1)
        def _():
            for i, rows in enumerate(blocks):
                tr, ti = window(k, 0, i, row_offset)
                vr, vi = zrecv[k, 0, rows, :].astype(F32), zrecv[k, 1, rows, :].astype(F32)
                x_v[0, rows, :], x_v[1, rows, :] = times(tr, ti, vr, vi)
                gr, gi = times(vr, vi, w2_v[k, 0, rows, :], w2_v[k, 1, rows, :])
                gbuf[k, 0, i, 0] = gr.astype(BF16)
                gbuf[k, 0, i, 1] = (-gi).astype(BF16)

        propagate(x_v, w3_v, tab)
        for i, rows in enumerate(blocks):
            gr, gi = times(w1_v[k, 0, rows, :], w1_v[k, 1, rows, :], w3_v[0, rows, :], w3_v[1, rows, :])
            gbuf[k, 1, i, 0] = gr.astype(BF16)
            gbuf[k, 1, i, 1] = (-gi).astype(BF16)
        for d in (4, 3, 2, 1):
            g_start(k, 1, d)

        @pl.when(z == 0)
        def _():
            for i, rows in enumerate(blocks):
                tr, ti = window(k, 1, i, row_offset)
                x_v[0, rows, :], x_v[1, rows, :] = times(tr, ti, w3_v[0, rows, :], w3_v[1, rows, :])
            propagate(x_v, w4_v, tab)
            for i, rows in enumerate(blocks):
                wr, wi = w4_v[0, rows, :], w4_v[1, rows, :]
                gr, gi = times(start_v[k, 0, rows, :], start_v[k, 1, rows, :], wr, wi)
                gbuf[k, 0, i, 0] = gr.astype(BF16)
                gbuf[k, 0, i, 1] = (-gi).astype(BF16)

        for d in (4, 3, 2, 1):
            g_start(k, 0, d)
        g_sibling(k).start()
        g_local(k).start()

        @pl.when(z == 0)
        def _():
            for i, rows in enumerate(blocks):
                tr, ti = window(k, 0, i, row_offset)
                vr, vi = times(tr, ti, w4_v[0, rows, :], w4_v[1, rows, :])
                x_v[0, rows, :], x_v[1, rows, :] = vr, -vi
            back_rows, back_cols = (SIDE - row_offset) & (SIDE - 1), (SIDE - col_offset) & (SIDE - 1)
            for ri in range(2):
                moved = roll(x_v[ri], back_rows, back_cols)
                total_v[ri] = jnp.where(k > 0, total_v[ri], 0.0) + moved

    def position(k, carry):
        first_half(k)

        @pl.when(k == 0)
        def _():
            forward_windows(1)

        @pl.when(k == 1)
        def _():
            forward_pieces(0)

        second_half(k)
        return carry

    forward_windows(0)
    lax.fori_loop(0, PER, position, 0)

    def p_copy(half):
        rows = pl.ds(pl.multiple_of((2 * half + 1 - c) * STRIP, STRIP), STRIP)
        return pltpu.make_async_remote_copy(
            src_ref=total_v.at[:, rows, :], dst_ref=part_r.at[half], send_sem=p_send.at[half],
            recv_sem=p_recv.at[half], device_id=at(q + 1 - 2 * c, j), device_id_type=MESH)

    def rs_copy(i):
        return pltpu.make_async_remote_copy(
            src_ref=rs_s.at[lax.rem(member + i, group)], dst_ref=rs_r.at[member], send_sem=rs_send.at[i],
            recv_sem=rs_recv.at[i], device_id=at(q, mate(i)), device_id_type=MESH)

    def ar_copy(half, i):
        return pltpu.make_async_remote_copy(
            src_ref=ar_s.at[half], dst_ref=ar_r.at[level], send_sem=ar_send.at[half, i],
            recv_sem=ar_recv.at[i], device_id=at(c + 2 * half, tier(i)), device_id_type=MESH)

    def ag_copy(i):
        return pltpu.make_async_remote_copy(
            src_ref=probe_out.at[member], dst_ref=probe_out.at[member], send_sem=ag_send.at[i],
            recv_sem=ag_recv.at[i], device_id=at(q, mate(i)), device_id_type=MESH)

    @pl.when(z == 0)
    def _():
        for half in range(2):
            p_copy(half).start()
        for half in range(2):
            p_copy(half).wait()
            rows = pl.ds(pl.multiple_of((2 * half + c) * STRIP, STRIP), STRIP)
            block_sum = total_v[:, rows, :] + part_r[half]
            rs_s[:, half] = block_sum.reshape(rs_s.shape[:1] + rs_s.shape[2:])
        for i in range(1, group):
            rs_copy(i).start()
        rs_r[member] = rs_s[member]

    forward_pieces(1)

    @pl.when(z == 0)
    def _():
        for i in range(1, group):
            rs_copy(i).wait_recv()
        plane_sum = rs_r[0]
        for m in range(1, group):
            plane_sum = plane_sum + rs_r[m]
        ar_s[...] = plane_sum
        ar_r[level] = plane_sum[0]
        for i in range(hi_count):
            ar_copy(1, i).start()
        for i in range(1, hi_count):
            ar_copy(0, i).start()

    @pl.when(z == 1)
    def _():
        ar_copy(1, 0).wait_recv()

    for i in range(1, hi_count):
        ar_copy(0, i).wait_recv()
    piece_sum = ar_r[0]
    for m in range(1, hi_count):
        piece_sum = piece_sum + ar_r[m]
    probe_out[member] = piece_sum
    for i in range(1, group):
        ag_copy(i).start()
    for i in range(1, group):
        ag_copy(i).wait()

    for copy in idx_copies:
        copy.wait_send()

    @pl.when(z == 0)
    def _():
        for i in range(1, group):
            rs_copy(i).wait_send()
        for i in range(hi_count):
            ar_copy(1, i).wait_send()
        for i in range(1, hi_count):
            ar_copy(0, i).wait_send()

    def drain(k, carry):
        z_copy(k).wait_send()
        t_sibling(k).wait_send()
        g_sibling(k).wait_send()
        g_local(k).wait()
        g_arrival(k, 1 - c, 0).wait_recv()

        def act(arrival, onward):
            onward.wait_send()

        t_forward(k, act)
        g_forward(k, act)
        for d in range(1, RIM + 1):
            for b in range(2):
                t_copy(k, d, b, region(-d)).wait_send()
                g_copy(k, b, d, region(d)).wait_send()
                g_arrival(k, b, d).wait_recv()
        return carry

    lax.fori_loop(0, PER, drain, 0)


def main_call(transmission, probe, exit_adjoint, idx):
    n_scan = lax.axis_size("scan")
    across = 4 if n_scan == 64 else 2
    group = RIM * across
    hi_count = n_scan // group
    piece = (16 // group, 8, SIDE)
    hbm_spec = pl.BlockSpec(memory_space=pltpu.HBM)
    vmem_spec = pl.BlockSpec(memory_space=pltpu.VMEM)
    field = (2, SIDE, SIDE)
    dma = pltpu.SemaphoreType.DMA
    columns = transmission.shape[3]
    return pl.pallas_call(
        functools.partial(main_kernel, across, hi_count, n_scan),
        out_shape=(
            jax.ShapeDtypeStruct((PER, 2, RIM + 1, 2, STRIP, SIDE), BF16),
            jax.ShapeDtypeStruct((RIM + 1, 8, 128), jnp.int32),
            jax.ShapeDtypeStruct((group,) + piece, F32),
        ),
        in_specs=[hbm_spec] * 5,
        out_specs=(hbm_spec, hbm_spec, vmem_spec),
        scratch_shapes=[
            pltpu.VMEM((columns // HALF, 2, STRIP, HALF), F32),
            pltpu.VMEM((2, 2, 2, SIDE, SIDE), BF16),
            pltpu.VMEM(field, F32),
            pltpu.VMEM((PER,) + field, F32),
            pltpu.SMEM((RIM + 1, 8, 128), jnp.int32),
            pltpu.VMEM((PER, RIM + 1, 2, 2, STRIP, SIDE), BF16),
            pltpu.VMEM((PER, 2, RIM + 1, 2, STRIP, SIDE), BF16),
            pltpu.VMEM(field, F32),
            pltpu.VMEM((PER,) + field, F32),
            pltpu.VMEM((PER,) + field, F32),
            pltpu.VMEM((PER,) + field, F32),
            pltpu.VMEM(field, F32),
            pltpu.VMEM(field, F32),
            pltpu.VMEM((PER,) + field, BF16),
            pltpu.VMEM((PER,) + field, BF16),
            pltpu.VMEM((PER, RIM + 1, 2, STRIP, SIDE), BF16),
            pltpu.VMEM((PER, RIM + 1, 2, STRIP, SIDE), BF16),
            pltpu.VMEM((PER, 2, RIM, 2, STRIP, SIDE), BF16),
            pltpu.VMEM(field, F32),
            pltpu.VMEM((2, 2, STRIP, SIDE), F32),
            pltpu.VMEM((group, 2) + piece, F32),
            pltpu.VMEM((group, 2) + piece, F32),
            pltpu.VMEM((2,) + piece, F32),
            pltpu.VMEM((hi_count,) + piece, F32),
            dma((6,)),
            dma((columns // HALF,)),
            dma((RIM + 1,)),
            dma((RIM + 1,)),
            dma((PER, RIM + 1, 2)),
            dma((PER, 2, RIM + 1)),
            dma((PER, RIM + 1)),
            dma((PER, RIM + 1)),
            dma((PER,)),
            dma((PER,)),
            dma((PER, 2, RIM + 1)),
            dma((PER, 2, RIM + 1)),
            dma((PER, RIM + 1)),
            dma((PER, RIM + 1)),
            dma((2,)),
            dma((2,)),
            dma((group,)),
            dma((group,)),
            dma((2, hi_count)),
            dma((hi_count,)),
            dma((group,)),
            dma((group,)),
        ],
        compiler_params=pltpu.CompilerParams(
            collective_id=0, has_side_effects=True, vmem_limit_bytes=62 * 1024 * 1024
        ),
        cost_estimate=pl.CostEstimate(flops=8 * 12 * 2 * SIDE**3, bytes_accessed=8 << 20, transcendentals=0),
        name="waves",
    )(transmission, probe, exit_adjoint, jnp.asarray(tables()), idx)


def deposit_kernel(idx, pieces, probe_in, grad, probe_out):
    probe_out[...] = probe_in[...]
    grad[...] = jnp.zeros_like(grad)
    lane = lax.broadcasted_iota(jnp.int32, (1, 1, HALF), 2)
    row = lax.broadcasted_iota(jnp.int32, (1, STRIP, 1), 1)

    def add(n, carry):
        d = n // 4
        core = (n // 2) % 2
        k = n % 2
        row_offset = idx[d, core, k] & (STRIP - 1)
        col = idx[d, 2 + core, k]
        block = lax.shift_right_logical(col, 7)
        col_offset = col & (HALF - 1)
        low = jnp.where(d == 0, row_offset, 0)
        high = jnp.where(d == RIM, row_offset, STRIP)
        keep = (row >= low) & (row < high)
        piece = jnp.where(keep, pieces[k, core, d].astype(F32), 0.0)
        first, second = piece[:, :, :HALF], piece[:, :, HALF:]
        here = lane >= col_offset
        third_block = jnp.minimum(block + 2, grad.shape[3] // HALF - 1)
        for where_to, value in (
            (block, jnp.where(here, first, 0.0)),
            (block + 1, second),
            (third_block, jnp.where(here, 0.0, first)),
        ):
            cols = pl.ds(pl.multiple_of(where_to * HALF, HALF), HALF)
            grad[0, :, :, cols] = grad[0, :, :, cols] + value
        return carry

    lax.fori_loop(0, 4 * (RIM + 1), add, 0)


def deposit_call(idx_all, pieces, probe_sum, columns):
    vmem_spec = pl.BlockSpec(memory_space=pltpu.VMEM)
    return pl.pallas_call(
        deposit_kernel,
        out_shape=(
            jax.ShapeDtypeStruct((1, 2, STRIP, columns), F32),
            jax.ShapeDtypeStruct(probe_sum.shape, F32),
        ),
        in_specs=[pl.BlockSpec(memory_space=pltpu.SMEM), vmem_spec, vmem_spec],
        out_specs=(vmem_spec, vmem_spec),
        compiler_params=pltpu.CompilerParams(vmem_limit_bytes=62 * 1024 * 1024),
        name="deposit",
    )(idx_all, pieces, probe_sum)


def local(transmission, probe, exit_adjoint, scan_row, scan_col):
    idx = jnp.pad(jnp.concatenate([scan_row, scan_col], axis=0), ((0, 4), (0, 126)))
    pieces, idx_all, probe_sum = main_call(transmission, probe, exit_adjoint, idx)
    object_grad, probe_grad = deposit_call(idx_all, pieces, probe_sum, transmission.shape[3])
    return object_grad, probe_grad.reshape(2, STRIP, SIDE)


def solution(mesh):
    placed = (
        P("depth", None, "scan", None),
        P(),
        P(None, "scan", None, None, None),
        P(None, "scan"),
        P(None, "scan"),
    )
    return jax.shard_map(
        local,
        mesh=mesh,
        in_specs=placed,
        out_specs=(P("depth", None, "scan", None), P(None, "depth", None)),
        check_vma=False,
    )
```

```python
import functools
import math

import jax
import jax.numpy as jnp
import numpy as np
from jax import lax
from jax.experimental import pallas as pl
from jax.experimental.pallas import tpu as pltpu
from jax.sharding import PartitionSpec as P

FRESNEL = 0.25
SIDE = 256
HALF = SIDE // 2
STRIP = 64
RIM = SIDE // STRIP
BATCHES = 2
PER = 2
F32 = jnp.float32
BF16 = jnp.bfloat16
MESH = pl.DeviceIdType.MESH


def tables():
    k = np.arange(SIDE)
    f = np.where(k < HALF, k, k - SIDE).astype(np.float64)
    h = np.exp(-1j * math.pi * FRESNEL * f * f / SIDE)
    dft = np.exp(-2j * math.pi * (np.outer(k, k) % SIDE) / SIDE)
    a = (dft.conj() / SIDE) @ (h[:, None] * dft)
    lefts, rights = [], []
    for sign in (1.0, -1.0):
        m = (a[:HALF, :HALF] + sign * a[:HALF, HALF:]) / 2.0
        left = np.block([[m.real, -m.imag], [m.imag, m.real]]).astype(np.float32)
        for out, full in ((lefts, left), (rights, left.T.copy())):
            high = full.astype(jnp.bfloat16)
            low = (full - high.astype(np.float32)).astype(jnp.bfloat16)
            out.append(np.stack([high, low]))
    return np.stack([np.stack(lefts), np.stack(rights)])


def dot(a, b):
    return jnp.dot(a, b, preferred_element_type=F32)


def split(x):
    high = x.astype(BF16)
    return high, (x - high.astype(F32)).astype(BF16)


def propagate(x_ref, w_ref, tab):
    middle = []
    for a in range(2):
        parts = []
        for ri in range(2):
            top, low = x_ref[ri, :HALF, :], x_ref[ri, HALF:, :]
            v = top + low if a == 0 else top - low
            l, r = v[:, :HALF], v[:, HALF:]
            parts.append(jnp.concatenate([l + r, l - r], axis=1))
        high, low = split(jnp.concatenate(parts, axis=0))
        left_high, left_low = tab[0, a, 0], tab[0, a, 1]
        middle.append(dot(left_high, high) + dot(left_low, high) + dot(left_high, low))
    sectors = []
    for b in range(2):
        cols = slice(b * HALF, (b + 1) * HALF)
        rows = [jnp.concatenate([z[:HALF, cols], z[HALF:, cols]], axis=1) for z in middle]
        high, low = split(jnp.concatenate(rows, axis=0))
        right_high, right_low = tab[1, b, 0], tab[1, b, 1]
        sectors.append(dot(high, right_high) + dot(high, right_low) + dot(low, right_high))
    for ri in range(2):
        cols = slice(ri * HALF, (ri + 1) * HALF)
        for half_col in range(2):
            s, d = sectors[0][:, cols], sectors[1][:, cols]
            v = s + d if half_col == 0 else s - d
            out = slice(half_col * HALF, (half_col + 1) * HALF)
            w_ref[ri, :HALF, out] = v[:HALF] + v[HALF:]
            w_ref[ri, HALF:, out] = v[:HALF] - v[HALF:]


def times(ar, ai, br, bi):
    return ar * br - ai * bi, ar * bi + ai * br


def main_kernel(
    across, hi_count, n_scan,
    trans, probe, exit_adjoint, table_in, idx_in,
    pieces, idx_all, probe_out,
    strip, tab, probe_v, exit_v, idx_s,
    xsend, xrecv, sbuf, tbuf, x_v, start_v, w1_v, w2_v, w3_v, w4_v, zsend, zrecv,
    t_transit, g_transit, gbuf, total_v, part_r, rs_s, rs_r, ar_s, ar_r,
    local_sems, strip_sems, x_send, x_recv, idx_send, idx_recv, t_send, t_recv, tt_send, tt_recv, z_send, z_recv,
    g_send, g_recv, gt_send, gt_recv, p_send, p_recv, rs_send, rs_recv, ar_send, ar_recv, ag_send, ag_recv,
):
    q = lax.axis_index("depth")
    j = lax.axis_index("scan")
    z = q // 2
    c = q % 2
    group = RIM * across
    member = j % group
    level = j // group
    y = j % RIM
    x = member // RIM
    span = RIM * (across - 1)

    def at(depth, scan):
        return {"depth": depth, "scan": scan}

    def region(step):
        return lax.rem(j + step + n_scan, n_scan)

    def strip_of(core, e):
        return e + core * (RIM - 2 * e)

    def both(sign, plus, minus):
        return ((sign > 0) & plus) | ((sign < 0) & minus)

    def turns(sign, e):
        return both(sign, y + e >= RIM, y < e)

    def turned_here(sign, e):
        return both(sign, y < e, y >= RIM - e)

    def leaves(sign):
        return both(sign, x == across - 1, x == 0)

    def left_here(sign):
        return both(sign, x == 0, x == across - 1)

    def mate(i):
        return level * group + lax.rem(member + i, group)

    def tier(i):
        return lax.rem(level + i, hi_count) * group + member

    loads = [
        pltpu.make_async_copy(table_in, tab, local_sems.at[1]),
        pltpu.make_async_copy(probe, probe_v, local_sems.at[2]),
        pltpu.make_async_copy(exit_adjoint.at[c], exit_v, local_sems.at[3]),
        pltpu.make_async_copy(idx_in, idx_all.at[0], local_sems.at[4]),
    ]

    def strip_copy(i):
        cols = pl.ds(pl.multiple_of(i * HALF, HALF), HALF)
        return pltpu.make_async_copy(trans.at[0, :, :, cols], strip.at[i], strip_sems.at[i])

    for copy in loads:
        copy.start()

    def start_strip(i, carry):
        strip_copy(i).start()
        return carry

    def wait_strip(i, carry):
        strip_copy(i).wait()
        return carry

    lax.fori_loop(0, strip.shape[0], start_strip, 0)

    barrier = pltpu.get_barrier_semaphore()
    partners = [at(q + 1 - 2 * c, j), at(q + 2 - 4 * z, j)]
    for d in range(1, RIM + 1):
        for b in range(2):
            partners.append(at(2 * z + b, region(d)))
            partners.append(at(2 * z + b, region(-d)))
    for i in range(1, group):
        partners.append(at(q, mate(i)))
    for i in range(1, hi_count):
        partners.append(at(q, tier(i)))
        partners.append(at(q + 2 - 4 * z, tier(i)))
    for device in partners:
        pl.semaphore_signal(barrier, inc=1, device_id=device, device_id_type=MESH)
    crossing = ((x == 0, span), (x == across - 1, -span))
    for edge, step in crossing:
        @pl.when(edge)
        def _(step=step):
            pl.semaphore_signal(
                barrier, inc=1, device_id=at(q + 1 - 2 * c, region(step)), device_id_type=MESH)
    on_edge = ((x == 0) | (x == across - 1)).astype(jnp.int32)
    pl.semaphore_wait(barrier, len(partners) + on_edge)

    def x_copy(k):
        return pltpu.make_async_remote_copy(
            src_ref=xsend.at[k], dst_ref=xrecv.at[k], send_sem=x_send.at[k], recv_sem=x_recv.at[k],
            device_id=at(q, region(RIM)), device_id_type=MESH)

    idx_copies = [
        pltpu.make_async_remote_copy(
            src_ref=idx_in, dst_ref=idx_all.at[d], send_sem=idx_send.at[d], recv_sem=idx_recv.at[d],
            device_id=at(q, region(d)), device_id_type=MESH)
        for d in range(1, RIM + 1)
    ]
    for copy in idx_copies:
        copy.start()

    loads[2].wait()

    @pl.when((z == 1) & (c == 1))
    def _():
        for k in range(PER):
            xsend[k] = exit_v[k].astype(BF16)
            x_copy(k).start()

    loads[3].wait()
    for copy in idx_copies:
        copy.wait_recv()
    to_smem = pltpu.make_async_copy(idx_all, idx_s, local_sems.at[5])
    to_smem.start()
    to_smem.wait()
    lax.fori_loop(0, strip.shape[0], wait_strip, 0)

    lane = lax.broadcasted_iota(jnp.int32, (1, 1, HALF), 2)
    last_block = strip.shape[0] - 1

    def t_copy(k, d, b, target, entry=None):
        return pltpu.make_async_remote_copy(
            src_ref=sbuf.at[k, d, b],
            dst_ref=tbuf.at[k, c, d] if entry is None else t_transit.at[k, entry],
            send_sem=t_send.at[k, d, b],
            recv_sem=t_recv.at[k, c, d] if entry is None else tt_recv.at[k, entry],
            device_id=at(2 * z + b, target), device_id_type=MESH)

    def t_start(k, e, b):
        d, sign = strip_of(b, e), 2 * b - 1
        if e == RIM:
            detour, step, entry = leaves(sign), -sign * span, e - 1 + c
        else:
            detour, step, entry = turns(sign, e) & (c == b), -sign * (RIM - e), e - 1

        @pl.when(detour)
        def _():
            t_copy(k, d, b, region(step), entry).start()

        @pl.when(jnp.logical_not(detour))
        def _():
            t_copy(k, d, b, region(sign * e)).start()

    def t_onward(k, slot, e, entry, step):
        d = strip_of(c, e)
        return pltpu.make_async_remote_copy(
            src_ref=t_transit.at[k, entry], dst_ref=tbuf.at[k, slot, d],
            send_sem=tt_send.at[k, entry], recv_sem=t_recv.at[k, slot, d],
            device_id=at(q, region(step)), device_id_type=MESH)

    def t_transit_arrival(k, entry):
        return pltpu.make_async_remote_copy(
            src_ref=sbuf.at[k, 0, 0], dst_ref=t_transit.at[k, entry],
            send_sem=tt_send.at[k, entry], recv_sem=tt_recv.at[k, entry],
            device_id=at(q + 1 - 2 * c, j), device_id_type=MESH)

    def t_forward(k, act):
        sign = 2 * c - 1

        @pl.when(left_here(sign))
        def _():
            for slot in range(2):
                entry = RIM - 1 + slot
                act(t_transit_arrival(k, entry), t_onward(k, slot, RIM, entry, sign * RIM * across))

        for e in range(1, RIM):
            @pl.when(turned_here(sign, e))
            def _(e=e):
                act(t_transit_arrival(k, e - 1), t_onward(k, c, e, e - 1, sign * RIM))

    def t_sibling(k):
        d = RIM * (1 - c)
        return pltpu.make_async_remote_copy(
            src_ref=sbuf.at[k, d, 1 - c], dst_ref=tbuf.at[k, c, d],
            send_sem=t_send.at[k, d, 1 - c], recv_sem=t_recv.at[k, c, d],
            device_id=at(q + 1 - 2 * c, j), device_id_type=MESH)

    def t_local(k):
        d = RIM * c
        return pltpu.make_async_copy(sbuf.at[k, d, c], tbuf.at[k, c, d], t_send.at[k, d, c])

    def t_arrival(k, slot, d):
        return pltpu.make_async_remote_copy(
            src_ref=sbuf.at[k, 0, 0], dst_ref=tbuf.at[k, slot, d],
            send_sem=t_send.at[k, d, 0], recv_sem=t_recv.at[k, slot, d],
            device_id=at(q + 1 - 2 * c, j), device_id_type=MESH)

    def send_windows(k):
        for e in (4, 3, 2, 1, 0):
            for b in range(2):
                d = strip_of(b, e)
                col = idx_s[d, 2 + b, k]
                block = lax.shift_right_logical(col, 7)
                offset = col & (HALF - 1)
                first, second = strip[block], strip[block + 1]
                third = strip[jnp.minimum(block + 2, last_block)]
                sbuf[k, d, b, :, :, :HALF] = jnp.where(lane >= offset, first, third).astype(BF16)
                sbuf[k, d, b, :, :, HALF:] = second.astype(BF16)
                if e > 0:
                    t_start(k, e, b)
        t_sibling(k).start()
        t_local(k).start()

    send_windows(0)

    def wait_windows(k):
        t_local(k).wait()
        t_arrival(k, 1 - c, RIM * c).wait_recv()
        for e in range(1, RIM + 1):
            for slot in range(2):
                t_arrival(k, slot, strip_of(c, e)).wait_recv()

    row = lax.broadcasted_iota(jnp.int32, (STRIP, 1), 0)

    def offsets(k):
        return idx_s[RIM * c, c, k] & (STRIP - 1), idx_s[RIM * c, 2 + c, k] & (HALF - 1)

    def window(k, slot, block, row_offset):
        if block > 0:
            return tbuf[k, slot, block, 0].astype(F32), tbuf[k, slot, block, 1].astype(F32)
        here = row >= row_offset
        return tuple(
            jnp.where(here, tbuf[k, slot, 0, ri].astype(F32), tbuf[k, slot, RIM, ri].astype(F32))
            for ri in range(2)
        )

    blocks = [slice(i * STRIP, (i + 1) * STRIP) for i in range(RIM)]

    def roll(x, rows, cols):
        return pltpu.roll(pltpu.roll(x, rows, 0), cols, 1)

    def z_copy(k):
        return pltpu.make_async_remote_copy(
            src_ref=zsend.at[k], dst_ref=zrecv.at[k], send_sem=z_send.at[k], recv_sem=z_recv.at[k],
            device_id=at(q + 2 - 4 * z, j), device_id_type=MESH)

    for copy in loads[:2]:
        copy.wait()

    def send_later(k):
        @pl.when(k == 0)
        def _():
            send_windows(1)

    def first_half(k):
        row_offset, col_offset = offsets(k)

        @pl.when(z == 0)
        def _():
            for ri in range(2):
                start_v[k, ri] = roll(probe_v[ri], row_offset, col_offset)
            wait_windows(k)
            send_later(k)
            for i, rows in enumerate(blocks):
                tr, ti = window(k, 0, i, row_offset)
                x_v[0, rows, :], x_v[1, rows, :] = times(tr, ti, start_v[k, 0, rows, :], start_v[k, 1, rows, :])

        @pl.when(z == 1)
        def _():
            @pl.when(c == 0)
            def _():
                x_v[...] = exit_v[k]

            @pl.when(c == 1)
            def _():
                x_copy(k).wait_recv()
                x_v[...] = xrecv[k].astype(F32)

            x_v[0] = roll(x_v[0], row_offset, col_offset)
            x_v[1] = -roll(x_v[1], row_offset, col_offset)

        propagate(x_v, w1_v.at[k], tab)

        @pl.when(z == 1)
        def _():
            wait_windows(k)
            send_later(k)

        for i, rows in enumerate(blocks):
            tr, ti = window(k, 1, i, row_offset)
            x_v[0, rows, :], x_v[1, rows, :] = times(tr, ti, w1_v[k, 0, rows, :], w1_v[k, 1, rows, :])
        propagate(x_v, w2_v.at[k], tab)

        @pl.when(z == 0)
        def _():
            zsend[k] = w2_v[k].astype(BF16)

        @pl.when(z == 1)
        def _():
            for i, rows in enumerate(blocks):
                tr, ti = window(k, 0, i, row_offset)
                vr, vi = times(tr, ti, w2_v[k, 0, rows, :], w2_v[k, 1, rows, :])
                zsend[k, 0, rows, :] = vr.astype(BF16)
                zsend[k, 1, rows, :] = vi.astype(BF16)

        z_copy(k).start()

    def forward_windows(k):
        def act(arrival, onward):
            arrival.wait_recv()
            onward.start()
        t_forward(k, act)


    def g_copy(k, slot, e, target, entry=None):
        d = strip_of(c, e)
        return pltpu.make_async_remote_copy(
            src_ref=gbuf.at[k, slot, lax.rem(d, RIM)],
            dst_ref=pieces.at[k, c, d] if entry is None else g_transit.at[k, entry],
            send_sem=g_send.at[k, slot, e],
            recv_sem=g_recv.at[k, c, d] if entry is None else gt_recv.at[k, entry],
            device_id=at(2 * z + slot, target), device_id_type=MESH)

    def g_start(k, slot, e):
        sign = 1 - 2 * c
        if e == RIM:
            detour, step, entry = leaves(sign), -sign * span, e - 1 + c
        else:
            detour, step, entry = turns(sign, e) & (c == slot), -sign * (RIM - e), e - 1

        @pl.when(detour)
        def _():
            g_copy(k, slot, e, region(step), entry).start()

        @pl.when(jnp.logical_not(detour))
        def _():
            g_copy(k, slot, e, region(sign * e)).start()

    def g_onward(k, core, d, entry, step):
        return pltpu.make_async_remote_copy(
            src_ref=g_transit.at[k, entry], dst_ref=pieces.at[k, core, d],
            send_sem=gt_send.at[k, entry], recv_sem=g_recv.at[k, core, d],
            device_id=at(q, region(step)), device_id_type=MESH)

    def g_transit_arrival(k, entry):
        return pltpu.make_async_remote_copy(
            src_ref=gbuf.at[k, 0, 0], dst_ref=g_transit.at[k, entry],
            send_sem=gt_send.at[k, entry], recv_sem=gt_recv.at[k, entry],
            device_id=at(q + 1 - 2 * c, j), device_id_type=MESH)

    def g_forward(k, act):
        for core in range(2):
            @pl.when(left_here(1 - 2 * core))
            def _(core=core):
                entry, step = RIM - 1 + core, (1 - 2 * core) * RIM * across
                act(g_transit_arrival(k, entry), g_onward(k, core, strip_of(core, RIM), entry, step))

        sign = 1 - 2 * c
        for e in range(1, RIM):
            @pl.when(turned_here(sign, e))
            def _(e=e):
                act(g_transit_arrival(k, e - 1), g_onward(k, c, strip_of(c, e), e - 1, sign * RIM))

    def forward_pieces(k):
        def act(arrival, onward):
            arrival.wait_recv()
            onward.start()
        g_forward(k, act)

    def g_sibling(k):
        return pltpu.make_async_remote_copy(
            src_ref=gbuf.at[k, 1 - c, 0], dst_ref=pieces.at[k, c, RIM * c],
            send_sem=g_send.at[k, 1, 0], recv_sem=g_recv.at[k, c, RIM * c],
            device_id=at(q + 1 - 2 * c, j), device_id_type=MESH)

    def g_local(k):
        return pltpu.make_async_copy(gbuf.at[k, c, 0], pieces.at[k, c, RIM * c], g_send.at[k, 0, 0])

    def g_arrival(k, core, d):
        return pltpu.make_async_remote_copy(
            src_ref=gbuf.at[k, 0, 0], dst_ref=pieces.at[k, core, d],
            send_sem=g_send.at[k, 0, d], recv_sem=g_recv.at[k, core, d],
            device_id=at(q + 1 - 2 * c, j), device_id_type=MESH)

    def second_half(k):
        row_offset, col_offset = offsets(k)
        z_copy(k).wait_recv()

        @pl.when(z == 0)
        def _():
            x_v[...] = zrecv[k].astype(F32)

        @pl.when(z == 1)
        def _():
            for i, rows in enumerate(blocks):
                tr, ti = window(k, 0, i, row_offset)
                vr, vi = zrecv[k, 0, rows, :].astype(F32), zrecv[k, 1, rows, :].astype(F32)
                x_v[0, rows, :], x_v[1, rows, :] = times(tr, ti, vr, vi)
                gr, gi = times(vr, vi, w2_v[k, 0, rows, :], w2_v[k, 1, rows, :])
                gbuf[k, 0, i, 0] = gr.astype(BF16)
                gbuf[k, 0, i, 1] = (-gi).astype(BF16)

        propagate(x_v, w3_v, tab)
        for i, rows in enumerate(blocks):
            gr, gi = times(w1_v[k, 0, rows, :], w1_v[k, 1, rows, :], w3_v[0, rows, :], w3_v[1, rows, :])
            gbuf[k, 1, i, 0] = gr.astype(BF16)
            gbuf[k, 1, i, 1] = (-gi).astype(BF16)
        for d in (4, 3, 2, 1):
            g_start(k, 1, d)

        @pl.when(z == 0)
        def _():
            for i, rows in enumerate(blocks):
                tr, ti = window(k, 1, i, row_offset)
                x_v[0, rows, :], x_v[1, rows, :] = times(tr, ti, w3_v[0, rows, :], w3_v[1, rows, :])
            propagate(x_v, w4_v, tab)
            for i, rows in enumerate(blocks):
                wr, wi = w4_v[0, rows, :], w4_v[1, rows, :]
                gr, gi = times(start_v[k, 0, rows, :], start_v[k, 1, rows, :], wr, wi)
                gbuf[k, 0, i, 0] = gr.astype(BF16)
                gbuf[k, 0, i, 1] = (-gi).astype(BF16)

        for d in (4, 3, 2, 1):
            g_start(k, 0, d)
        g_sibling(k).start()
        g_local(k).start()

        @pl.when(z == 0)
        def _():
            for i, rows in enumerate(blocks):
                tr, ti = window(k, 0, i, row_offset)
                vr, vi = times(tr, ti, w4_v[0, rows, :], w4_v[1, rows, :])
                x_v[0, rows, :], x_v[1, rows, :] = vr, -vi
            back_rows, back_cols = (SIDE - row_offset) & (SIDE - 1), (SIDE - col_offset) & (SIDE - 1)
            for ri in range(2):
                moved = roll(x_v[ri], back_rows, back_cols)
                total_v[ri] = jnp.where(k > 0, total_v[ri], 0.0) + moved

    def position(k, carry):
        first_half(k)

        @pl.when(k == 0)
        def _():
            forward_windows(1)

        @pl.when(k == 1)
        def _():
            forward_pieces(0)

        second_half(k)
        return carry

    forward_windows(0)
    lax.fori_loop(0, PER, position, 0)

    def p_copy(half):
        rows = pl.ds(pl.multiple_of((2 * half + 1 - c) * STRIP, STRIP), STRIP)
        return pltpu.make_async_remote_copy(
            src_ref=total_v.at[:, rows, :], dst_ref=part_r.at[half], send_sem=p_send.at[half],
            recv_sem=p_recv.at[half], device_id=at(q + 1 - 2 * c, j), device_id_type=MESH)

    def rs_copy(i):
        return pltpu.make_async_remote_copy(
            src_ref=rs_s.at[lax.rem(member + i, group)], dst_ref=rs_r.at[member], send_sem=rs_send.at[i],
            recv_sem=rs_recv.at[i], device_id=at(q, mate(i)), device_id_type=MESH)

    def ar_copy(half, i):
        return pltpu.make_async_remote_copy(
            src_ref=ar_s.at[half], dst_ref=ar_r.at[level], send_sem=ar_send.at[half, i],
            recv_sem=ar_recv.at[i], device_id=at(c + 2 * half, tier(i)), device_id_type=MESH)

    def ag_copy(i):
        return pltpu.make_async_remote_copy(
            src_ref=probe_out.at[member], dst_ref=probe_out.at[member], send_sem=ag_send.at[i],
            recv_sem=ag_recv.at[i], device_id=at(q, mate(i)), device_id_type=MESH)

    @pl.when(z == 0)
    def _():
        for half in range(2):
            p_copy(half).start()
        for half in range(2):
            p_copy(half).wait()
            rows = pl.ds(pl.multiple_of((2 * half + c) * STRIP, STRIP), STRIP)
            block_sum = total_v[:, rows, :] + part_r[half]
            rs_s[:, half] = block_sum.reshape(rs_s.shape[:1] + rs_s.shape[2:])
        for i in range(1, group):
            rs_copy(i).start()
        rs_r[member] = rs_s[member]

    forward_pieces(1)

    @pl.when(z == 0)
    def _():
        for i in range(1, group):
            rs_copy(i).wait_recv()
        plane_sum = rs_r[0]
        for m in range(1, group):
            plane_sum = plane_sum + rs_r[m]
        ar_s[...] = plane_sum
        ar_r[level] = plane_sum[0]
        for i in range(hi_count):
            ar_copy(1, i).start()
        for i in range(1, hi_count):
            ar_copy(0, i).start()

    @pl.when(z == 1)
    def _():
        ar_copy(1, 0).wait_recv()

    for i in range(1, hi_count):
        ar_copy(0, i).wait_recv()
    piece_sum = ar_r[0]
    for m in range(1, hi_count):
        piece_sum = piece_sum + ar_r[m]
    probe_out[member] = piece_sum
    for i in range(1, group):
        ag_copy(i).start()
    for i in range(1, group):
        ag_copy(i).wait()

    for copy in idx_copies:
        copy.wait_send()

    @pl.when(z == 0)
    def _():
        for i in range(1, group):
            rs_copy(i).wait_send()
        for i in range(hi_count):
            ar_copy(1, i).wait_send()
        for i in range(1, hi_count):
            ar_copy(0, i).wait_send()

    def drain(k, carry):
        z_copy(k).wait_send()
        t_sibling(k).wait_send()
        g_sibling(k).wait_send()
        g_local(k).wait()
        g_arrival(k, 1 - c, RIM * (1 - c)).wait_recv()

        def act(arrival, onward):
            onward.wait_send()

        t_forward(k, act)
        g_forward(k, act)
        for e in range(1, RIM + 1):
            for b in range(2):
                d = strip_of(b, e)
                t_copy(k, d, b, region(e)).wait_send()
                g_copy(k, b, e, region(e)).wait_send()
                g_arrival(k, b, d).wait_recv()

        @pl.when((z == 1) & (c == 1))
        def _():
            x_copy(k).wait_send()

        return carry

    lax.fori_loop(0, PER, drain, 0)


def main_call(transmission, probe, exit_adjoint, idx):
    n_scan = lax.axis_size("scan")
    across = 4 if n_scan == 64 else 2
    group = RIM * across
    hi_count = n_scan // group
    piece = (16 // group, 8, SIDE)
    hbm_spec = pl.BlockSpec(memory_space=pltpu.HBM)
    vmem_spec = pl.BlockSpec(memory_space=pltpu.VMEM)
    field = (2, SIDE, SIDE)
    dma = pltpu.SemaphoreType.DMA
    columns = transmission.shape[3]
    return pl.pallas_call(
        functools.partial(main_kernel, across, hi_count, n_scan),
        out_shape=(
            jax.ShapeDtypeStruct((PER, 2, RIM + 1, 2, STRIP, SIDE), BF16),
            jax.ShapeDtypeStruct((RIM + 1, 8, 128), jnp.int32),
            jax.ShapeDtypeStruct((group,) + piece, F32),
        ),
        in_specs=[hbm_spec] * 5,
        out_specs=(hbm_spec, hbm_spec, vmem_spec),
        scratch_shapes=[
            pltpu.VMEM((columns // HALF, 2, STRIP, HALF), F32),
            pltpu.VMEM((2, 2, 2, SIDE, SIDE), BF16),
            pltpu.VMEM(field, F32),
            pltpu.VMEM((PER,) + field, F32),
            pltpu.SMEM((RIM + 1, 8, 128), jnp.int32),
            pltpu.VMEM((PER,) + field, BF16),
            pltpu.VMEM((PER,) + field, BF16),
            pltpu.VMEM((PER, RIM + 1, 2, 2, STRIP, SIDE), BF16),
            pltpu.VMEM((PER, 2, RIM + 1, 2, STRIP, SIDE), BF16),
            pltpu.VMEM(field, F32),
            pltpu.VMEM((PER,) + field, F32),
            pltpu.VMEM((PER,) + field, F32),
            pltpu.VMEM((PER,) + field, F32),
            pltpu.VMEM(field, F32),
            pltpu.VMEM(field, F32),
            pltpu.VMEM((PER,) + field, BF16),
            pltpu.VMEM((PER,) + field, BF16),
            pltpu.VMEM((PER, RIM + 1, 2, STRIP, SIDE), BF16),
            pltpu.VMEM((PER, RIM + 1, 2, STRIP, SIDE), BF16),
            pltpu.VMEM((PER, 2, RIM, 2, STRIP, SIDE), BF16),
            pltpu.VMEM(field, F32),
            pltpu.VMEM((2, 2, STRIP, SIDE), F32),
            pltpu.VMEM((group, 2) + piece, F32),
            pltpu.VMEM((group, 2) + piece, F32),
            pltpu.VMEM((2,) + piece, F32),
            pltpu.VMEM((hi_count,) + piece, F32),
            dma((6,)),
            dma((columns // HALF,)),
            dma((PER,)),
            dma((PER,)),
            dma((RIM + 1,)),
            dma((RIM + 1,)),
            dma((PER, RIM + 1, 2)),
            dma((PER, 2, RIM + 1)),
            dma((PER, RIM + 1)),
            dma((PER, RIM + 1)),
            dma((PER,)),
            dma((PER,)),
            dma((PER, 2, RIM + 1)),
            dma((PER, 2, RIM + 1)),
            dma((PER, RIM + 1)),
            dma((PER, RIM + 1)),
            dma((2,)),
            dma((2,)),
            dma((group,)),
            dma((group,)),
            dma((2, hi_count)),
            dma((hi_count,)),
            dma((group,)),
            dma((group,)),
        ],
        compiler_params=pltpu.CompilerParams(
            collective_id=0, has_side_effects=True, vmem_limit_bytes=62 * 1024 * 1024
        ),
        cost_estimate=pl.CostEstimate(flops=8 * 12 * 2 * SIDE**3, bytes_accessed=8 << 20, transcendentals=0),
        name="waves",
    )(transmission, probe, exit_adjoint, jnp.asarray(tables()), idx)


def deposit_kernel(idx, pieces, probe_in, grad, probe_out):
    probe_out[...] = probe_in[...]
    grad[...] = jnp.zeros_like(grad)
    lane = lax.broadcasted_iota(jnp.int32, (1, 1, HALF), 2)
    row = lax.broadcasted_iota(jnp.int32, (1, STRIP, 1), 1)

    def add(n, carry):
        d = n // 4
        core = (n // 2) % 2
        k = n % 2
        row_offset = idx[d, core, k] & (STRIP - 1)
        col = idx[d, 2 + core, k]
        block = lax.shift_right_logical(col, 7)
        col_offset = col & (HALF - 1)
        low = jnp.where(d == 0, row_offset, 0)
        high = jnp.where(d == RIM, row_offset, STRIP)
        keep = (row >= low) & (row < high)
        piece = jnp.where(keep, pieces[k, core, d].astype(F32), 0.0)
        first, second = piece[:, :, :HALF], piece[:, :, HALF:]
        here = lane >= col_offset
        third_block = jnp.minimum(block + 2, grad.shape[3] // HALF - 1)
        for where_to, value in (
            (block, jnp.where(here, first, 0.0)),
            (block + 1, second),
            (third_block, jnp.where(here, 0.0, first)),
        ):
            cols = pl.ds(pl.multiple_of(where_to * HALF, HALF), HALF)
            grad[0, :, :, cols] = grad[0, :, :, cols] + value
        return carry

    lax.fori_loop(0, 4 * (RIM + 1), add, 0)


def deposit_call(idx_all, pieces, probe_sum, columns):
    vmem_spec = pl.BlockSpec(memory_space=pltpu.VMEM)
    return pl.pallas_call(
        deposit_kernel,
        out_shape=(
            jax.ShapeDtypeStruct((1, 2, STRIP, columns), F32),
            jax.ShapeDtypeStruct(probe_sum.shape, F32),
        ),
        in_specs=[pl.BlockSpec(memory_space=pltpu.SMEM), vmem_spec, vmem_spec],
        out_specs=(vmem_spec, vmem_spec),
        compiler_params=pltpu.CompilerParams(vmem_limit_bytes=62 * 1024 * 1024),
        name="deposit",
    )(idx_all, pieces, probe_sum)


def local(transmission, probe, exit_adjoint, scan_row, scan_col):
    idx = jnp.pad(jnp.concatenate([scan_row, scan_col], axis=0), ((0, 4), (0, 126)))
    pieces, idx_all, probe_sum = main_call(transmission, probe, exit_adjoint, idx)
    object_grad, probe_grad = deposit_call(idx_all, pieces, probe_sum, transmission.shape[3])
    return object_grad, probe_grad.reshape(2, STRIP, SIDE)


def solution(mesh):
    placed = (
        P("depth", None, "scan", None),
        P(),
        P(None, "scan", None, None, None),
        P(None, "scan"),
        P(None, "scan"),
    )
    return jax.shard_map(
        local,
        mesh=mesh,
        in_specs=placed,
        out_specs=(P("depth", None, "scan", None), P(None, "depth", None)),
        check_vma=False,
    )
```

```python
import functools
import math

import jax
import jax.numpy as jnp
import numpy as np
from jax import lax
from jax.experimental import pallas as pl
from jax.experimental.pallas import tpu as pltpu
from jax.sharding import PartitionSpec as P

FRESNEL = 0.25
SIDE = 256
HALF = SIDE // 2
STRIP = 64
RIM = SIDE // STRIP
BATCHES = 2
PER = 2
F32 = jnp.float32
BF16 = jnp.bfloat16
MESH = pl.DeviceIdType.MESH


def tables():
    k = np.arange(SIDE)
    f = np.where(k < HALF, k, k - SIDE).astype(np.float64)
    h = np.exp(-1j * math.pi * FRESNEL * f * f / SIDE)
    dft = np.exp(-2j * math.pi * (np.outer(k, k) % SIDE) / SIDE)
    a = (dft.conj() / SIDE) @ (h[:, None] * dft)
    lefts, rights = [], []
    for sign in (1.0, -1.0):
        m = (a[:HALF, :HALF] + sign * a[:HALF, HALF:]) / 2.0
        left = np.block([[m.real, -m.imag], [m.imag, m.real]]).astype(np.float32)
        for out, full in ((lefts, left), (rights, left.T.copy())):
            high = full.astype(jnp.bfloat16)
            low = (full - high.astype(np.float32)).astype(jnp.bfloat16)
            out.append(np.stack([high, low]))
    return np.stack([np.stack(lefts), np.stack(rights)])


def dot(a, b):
    return jnp.dot(a, b, preferred_element_type=F32)


def split(x):
    high = x.astype(BF16)
    return high, (x - high.astype(F32)).astype(BF16)


def propagate(x_ref, w_ref, tab):
    middle = []
    for a in range(2):
        parts = []
        for ri in range(2):
            top, low = x_ref[ri, :HALF, :], x_ref[ri, HALF:, :]
            v = top + low if a == 0 else top - low
            l, r = v[:, :HALF], v[:, HALF:]
            parts.append(jnp.concatenate([l + r, l - r], axis=1))
        high, low = split(jnp.concatenate(parts, axis=0))
        left_high, left_low = tab[0, a, 0], tab[0, a, 1]
        middle.append(dot(left_high, high) + dot(left_low, high) + dot(left_high, low))
    sectors = []
    for b in range(2):
        cols = slice(b * HALF, (b + 1) * HALF)
        rows = [jnp.concatenate([z[:HALF, cols], z[HALF:, cols]], axis=1) for z in middle]
        high, low = split(jnp.concatenate(rows, axis=0))
        right_high, right_low = tab[1, b, 0], tab[1, b, 1]
        sectors.append(dot(high, right_high) + dot(high, right_low) + dot(low, right_high))
    for ri in range(2):
        cols = slice(ri * HALF, (ri + 1) * HALF)
        for half_col in range(2):
            s, d = sectors[0][:, cols], sectors[1][:, cols]
            v = s + d if half_col == 0 else s - d
            out = slice(half_col * HALF, (half_col + 1) * HALF)
            w_ref[ri, :HALF, out] = v[:HALF] + v[HALF:]
            w_ref[ri, HALF:, out] = v[:HALF] - v[HALF:]


def times(ar, ai, br, bi):
    return ar * br - ai * bi, ar * bi + ai * br


def main_kernel(
    across, hi_count, n_scan,
    trans, probe, exit_adjoint, table_in, row_in, col_in,
    pieces, idx_all, probe_out,
    strip, tab, probe_v, exit_v, idx_in, idx_v, idx_s,
    xsend, xrecv, sbuf, tbuf, x_v, start_v, w1_v, w2_v, w3_v, w4_v, zsend, zrecv,
    t_transit, g_transit, gbuf, total_v, part_r, rs_s, rs_r, ar_s, ar_r,
    local_sems, strip_sems, x_send, x_recv, idx_send, idx_recv, t_send, t_recv, tt_send, tt_recv, z_send, z_recv,
    g_send, g_recv, gt_send, gt_recv, p_send, p_recv, rs_send, rs_recv, ar_send, ar_recv, ag_send, ag_recv,
):
    q = lax.axis_index("depth")
    j = lax.axis_index("scan")
    z = q // 2
    c = q % 2
    group = RIM * across
    member = j % group
    level = j // group
    y = j % RIM
    x = member // RIM
    span = RIM * (across - 1)

    def at(depth, scan):
        return {"depth": depth, "scan": scan}

    def region(step):
        return lax.rem(j + step + n_scan, n_scan)

    def strip_of(core, e):
        return e + core * (RIM - 2 * e)

    def both(sign, plus, minus):
        return ((sign > 0) & plus) | ((sign < 0) & minus)

    def turns(sign, e):
        return both(sign, y + e >= RIM, y < e)

    def turned_here(sign, e):
        return both(sign, y < e, y >= RIM - e)

    def leaves(sign):
        return both(sign, x == across - 1, x == 0)

    def left_here(sign):
        return both(sign, x == 0, x == across - 1)

    def mate(i):
        return level * group + lax.rem(member + i, group)

    def tier(i):
        return lax.rem(level + i, hi_count) * group + member

    loads = [
        pltpu.make_async_copy(table_in, tab, local_sems.at[1]),
        pltpu.make_async_copy(probe, probe_v, local_sems.at[2]),
        pltpu.make_async_copy(exit_adjoint.at[c], exit_v, local_sems.at[3]),
    ]

    def strip_copy(i):
        cols = pl.ds(pl.multiple_of(i * HALF, HALF), HALF)
        return pltpu.make_async_copy(trans.at[0, :, :, cols], strip.at[i], strip_sems.at[i])

    for copy in loads:
        copy.start()

    def start_strip(i, carry):
        strip_copy(i).start()
        return carry

    def wait_strip(i, carry):
        strip_copy(i).wait()
        return carry

    lax.fori_loop(0, strip.shape[0], start_strip, 0)

    at_row = lax.broadcasted_iota(jnp.int32, (8, 128), 0)
    at_lane = lax.broadcasted_iota(jnp.int32, (8, 128), 1)
    own = jnp.zeros((8, 128), jnp.int32)
    for b in range(BATCHES):
        for k in range(PER):
            own = jnp.where((at_row == b) & (at_lane == k), row_in[b, k], own)
            own = jnp.where((at_row == 2 + b) & (at_lane == k), col_in[b, k], own)
    idx_in[...] = own
    idx_v[0] = own

    barrier = pltpu.get_barrier_semaphore()
    partners = [at(q + 1 - 2 * c, j), at(q + 2 - 4 * z, j)]
    for d in range(1, RIM + 1):
        for b in range(2):
            partners.append(at(2 * z + b, region(d)))
            partners.append(at(2 * z + b, region(-d)))
    for i in range(1, group):
        partners.append(at(q, mate(i)))
    for i in range(1, hi_count):
        partners.append(at(q, tier(i)))
        partners.append(at(q + 2 - 4 * z, tier(i)))
    for device in partners:
        pl.semaphore_signal(barrier, inc=1, device_id=device, device_id_type=MESH)
    crossing = ((x == 0, span), (x == across - 1, -span))
    for edge, step in crossing:
        @pl.when(edge)
        def _(step=step):
            pl.semaphore_signal(
                barrier, inc=1, device_id=at(q + 1 - 2 * c, region(step)), device_id_type=MESH)
    on_edge = ((x == 0) | (x == across - 1)).astype(jnp.int32)
    pl.semaphore_wait(barrier, len(partners) + on_edge)

    def x_copy(k):
        return pltpu.make_async_remote_copy(
            src_ref=xsend.at[k], dst_ref=xrecv.at[k], send_sem=x_send.at[k], recv_sem=x_recv.at[k],
            device_id=at(q, region(RIM)), device_id_type=MESH)

    idx_copies = [
        pltpu.make_async_remote_copy(
            src_ref=idx_in, dst_ref=idx_v.at[d], send_sem=idx_send.at[d], recv_sem=idx_recv.at[d],
            device_id=at(q, region(d)), device_id_type=MESH)
        for d in range(1, RIM + 1)
    ]
    for copy in idx_copies:
        copy.start()

    loads[2].wait()

    @pl.when((z == 1) & (c == 1))
    def _():
        for k in range(PER):
            xsend[k] = exit_v[k].astype(BF16)
        x_copy(0).start()

    for copy in idx_copies:
        copy.wait_recv()
    to_smem = pltpu.make_async_copy(idx_v, idx_s, local_sems.at[5])
    to_smem.start()
    to_all = pltpu.make_async_copy(idx_v, idx_all, local_sems.at[4])
    to_all.start()
    to_smem.wait()
    lax.fori_loop(0, strip.shape[0], wait_strip, 0)

    lane = lax.broadcasted_iota(jnp.int32, (1, 1, HALF), 2)
    last_block = strip.shape[0] - 1

    def t_copy(k, d, b, target, entry=None):
        return pltpu.make_async_remote_copy(
            src_ref=sbuf.at[k, d, b],
            dst_ref=tbuf.at[k, c, d] if entry is None else t_transit.at[k, entry],
            send_sem=t_send.at[k, d, b],
            recv_sem=t_recv.at[k, c, d] if entry is None else tt_recv.at[k, entry],
            device_id=at(2 * z + b, target), device_id_type=MESH)

    def t_start(k, e, b):
        d, sign = strip_of(b, e), 2 * b - 1
        if e == RIM:
            detour, step, entry = leaves(sign), -sign * span, e - 1 + c
        else:
            detour, step, entry = turns(sign, e) & (c == b), -sign * (RIM - e), e - 1

        @pl.when(detour)
        def _():
            t_copy(k, d, b, region(step), entry).start()

        @pl.when(jnp.logical_not(detour))
        def _():
            t_copy(k, d, b, region(sign * e)).start()

    def t_onward(k, slot, e, entry, step):
        d = strip_of(c, e)
        return pltpu.make_async_remote_copy(
            src_ref=t_transit.at[k, entry], dst_ref=tbuf.at[k, slot, d],
            send_sem=tt_send.at[k, entry], recv_sem=t_recv.at[k, slot, d],
            device_id=at(q, region(step)), device_id_type=MESH)

    def t_transit_arrival(k, entry):
        return pltpu.make_async_remote_copy(
            src_ref=sbuf.at[k, 0, 0], dst_ref=t_transit.at[k, entry],
            send_sem=tt_send.at[k, entry], recv_sem=tt_recv.at[k, entry],
            device_id=at(q + 1 - 2 * c, j), device_id_type=MESH)

    def t_forward(k, act):
        sign = 2 * c - 1

        for e in range(1, RIM):
            @pl.when(turned_here(sign, e))
            def _(e=e):
                act(t_transit_arrival(k, e - 1), t_onward(k, c, e, e - 1, sign * RIM))

        @pl.when(left_here(sign))
        def _():
            for slot in range(2):
                entry = RIM - 1 + slot
                act(t_transit_arrival(k, entry), t_onward(k, slot, RIM, entry, sign * RIM * across))

    def t_sibling(k):
        d = RIM * (1 - c)
        return pltpu.make_async_remote_copy(
            src_ref=sbuf.at[k, d, 1 - c], dst_ref=tbuf.at[k, c, d],
            send_sem=t_send.at[k, d, 1 - c], recv_sem=t_recv.at[k, c, d],
            device_id=at(q + 1 - 2 * c, j), device_id_type=MESH)

    def t_local(k):
        d = RIM * c
        return pltpu.make_async_copy(sbuf.at[k, d, c], tbuf.at[k, c, d], t_send.at[k, d, c])

    def t_arrival(k, slot, d):
        return pltpu.make_async_remote_copy(
            src_ref=sbuf.at[k, 0, 0], dst_ref=tbuf.at[k, slot, d],
            send_sem=t_send.at[k, d, 0], recv_sem=t_recv.at[k, slot, d],
            device_id=at(q + 1 - 2 * c, j), device_id_type=MESH)

    def send_windows(k):
        for e in (4, 3, 2, 1, 0):
            for b in range(2):
                d = strip_of(b, e)
                col = idx_s[d, 2 + b, k]
                block = lax.shift_right_logical(col, 7)
                offset = col & (HALF - 1)
                first, second = strip[block], strip[block + 1]
                third = strip[jnp.minimum(block + 2, last_block)]
                sbuf[k, d, b, :, :, :HALF] = jnp.where(lane >= offset, first, third).astype(BF16)
                sbuf[k, d, b, :, :, HALF:] = second.astype(BF16)
                if e > 0:
                    t_start(k, e, b)
        t_sibling(k).start()
        t_local(k).start()

    send_windows(0)

    @pl.when((z == 1) & (c == 1))
    def _():
        x_copy(1).start()


    def wait_windows(k):
        t_local(k).wait()
        t_arrival(k, 1 - c, RIM * c).wait_recv()
        for e in range(1, RIM + 1):
            for slot in range(2):
                t_arrival(k, slot, strip_of(c, e)).wait_recv()

    row = lax.broadcasted_iota(jnp.int32, (STRIP, 1), 0)

    def offsets(k):
        return idx_s[RIM * c, c, k] & (STRIP - 1), idx_s[RIM * c, 2 + c, k] & (HALF - 1)

    def window(k, slot, block, row_offset):
        if block > 0:
            return tbuf[k, slot, block, 0].astype(F32), tbuf[k, slot, block, 1].astype(F32)
        here = row >= row_offset
        return tuple(
            jnp.where(here, tbuf[k, slot, 0, ri].astype(F32), tbuf[k, slot, RIM, ri].astype(F32))
            for ri in range(2)
        )

    blocks = [slice(i * STRIP, (i + 1) * STRIP) for i in range(RIM)]

    def roll(x, rows, cols):
        return pltpu.roll(pltpu.roll(x, rows, 0), cols, 1)

    def z_copy(k):
        return pltpu.make_async_remote_copy(
            src_ref=zsend.at[k], dst_ref=zrecv.at[k], send_sem=z_send.at[k], recv_sem=z_recv.at[k],
            device_id=at(q + 2 - 4 * z, j), device_id_type=MESH)

    for copy in loads[:2]:
        copy.wait()

    def send_later(k):
        @pl.when(k == 0)
        def _():
            send_windows(1)

    def first_half(k):
        row_offset, col_offset = offsets(k)

        @pl.when(z == 0)
        def _():
            for ri in range(2):
                start_v[k, ri] = roll(probe_v[ri], row_offset, col_offset)
            wait_windows(k)
            send_later(k)
            for i, rows in enumerate(blocks):
                tr, ti = window(k, 0, i, row_offset)
                x_v[0, rows, :], x_v[1, rows, :] = times(tr, ti, start_v[k, 0, rows, :], start_v[k, 1, rows, :])

        @pl.when(z == 1)
        def _():
            @pl.when(c == 0)
            def _():
                x_v[...] = exit_v[k]

            @pl.when(c == 1)
            def _():
                x_copy(k).wait_recv()
                x_v[...] = xrecv[k].astype(F32)

            x_v[0] = roll(x_v[0], row_offset, col_offset)
            x_v[1] = -roll(x_v[1], row_offset, col_offset)

        propagate(x_v, w1_v.at[k], tab)

        @pl.when(z == 1)
        def _():
            wait_windows(k)
            send_later(k)

        for i, rows in enumerate(blocks):
            tr, ti = window(k, 1, i, row_offset)
            x_v[0, rows, :], x_v[1, rows, :] = times(tr, ti, w1_v[k, 0, rows, :], w1_v[k, 1, rows, :])
        propagate(x_v, w2_v.at[k], tab)

        @pl.when(z == 0)
        def _():
            zsend[k] = w2_v[k].astype(BF16)

        @pl.when(z == 1)
        def _():
            for i, rows in enumerate(blocks):
                tr, ti = window(k, 0, i, row_offset)
                vr, vi = times(tr, ti, w2_v[k, 0, rows, :], w2_v[k, 1, rows, :])
                zsend[k, 0, rows, :] = vr.astype(BF16)
                zsend[k, 1, rows, :] = vi.astype(BF16)

        z_copy(k).start()

    def forward_windows(k):
        def act(arrival, onward):
            arrival.wait_recv()
            onward.start()
        t_forward(k, act)


    def g_copy(k, slot, e, target, entry=None):
        d = strip_of(c, e)
        return pltpu.make_async_remote_copy(
            src_ref=gbuf.at[k, slot, lax.rem(d, RIM)],
            dst_ref=pieces.at[k, c, d] if entry is None else g_transit.at[k, entry],
            send_sem=g_send.at[k, slot, e],
            recv_sem=g_recv.at[k, c, d] if entry is None else gt_recv.at[k, entry],
            device_id=at(2 * z + slot, target), device_id_type=MESH)

    def g_start(k, slot, e):
        sign = 1 - 2 * c
        if e == RIM:
            detour, step, entry = leaves(sign), -sign * span, e - 1 + c
        else:
            detour, step, entry = turns(sign, e) & (c == slot), -sign * (RIM - e), e - 1

        @pl.when(detour)
        def _():
            g_copy(k, slot, e, region(step), entry).start()

        @pl.when(jnp.logical_not(detour))
        def _():
            g_copy(k, slot, e, region(sign * e)).start()

    def g_onward(k, core, d, entry, step):
        return pltpu.make_async_remote_copy(
            src_ref=g_transit.at[k, entry], dst_ref=pieces.at[k, core, d],
            send_sem=gt_send.at[k, entry], recv_sem=g_recv.at[k, core, d],
            device_id=at(q, region(step)), device_id_type=MESH)

    def g_transit_arrival(k, entry):
        return pltpu.make_async_remote_copy(
            src_ref=gbuf.at[k, 0, 0], dst_ref=g_transit.at[k, entry],
            send_sem=gt_send.at[k, entry], recv_sem=gt_recv.at[k, entry],
            device_id=at(q + 1 - 2 * c, j), device_id_type=MESH)

    def g_forward(k, act):
        for core in range(2):
            @pl.when(left_here(1 - 2 * core))
            def _(core=core):
                entry, step = RIM - 1 + core, (1 - 2 * core) * RIM * across
                act(g_transit_arrival(k, entry), g_onward(k, core, strip_of(core, RIM), entry, step))

        sign = 1 - 2 * c
        for e in range(1, RIM):
            @pl.when(turned_here(sign, e))
            def _(e=e):
                act(g_transit_arrival(k, e - 1), g_onward(k, c, strip_of(c, e), e - 1, sign * RIM))

    def forward_pieces(k):
        def act(arrival, onward):
            arrival.wait_recv()
            onward.start()
        g_forward(k, act)

    def g_sibling(k):
        return pltpu.make_async_remote_copy(
            src_ref=gbuf.at[k, 1 - c, 0], dst_ref=pieces.at[k, c, RIM * c],
            send_sem=g_send.at[k, 1, 0], recv_sem=g_recv.at[k, c, RIM * c],
            device_id=at(q + 1 - 2 * c, j), device_id_type=MESH)

    def g_local(k):
        return pltpu.make_async_copy(gbuf.at[k, c, 0], pieces.at[k, c, RIM * c], g_send.at[k, 0, 0])

    def g_arrival(k, core, d):
        return pltpu.make_async_remote_copy(
            src_ref=gbuf.at[k, 0, 0], dst_ref=pieces.at[k, core, d],
            send_sem=g_send.at[k, 0, d], recv_sem=g_recv.at[k, core, d],
            device_id=at(q + 1 - 2 * c, j), device_id_type=MESH)

    def second_half(k):
        row_offset, col_offset = offsets(k)
        z_copy(k).wait_recv()

        @pl.when(z == 0)
        def _():
            x_v[...] = zrecv[k].astype(F32)

        @pl.when(z == 1)
        def _():
            for i, rows in enumerate(blocks):
                tr, ti = window(k, 0, i, row_offset)
                vr, vi = zrecv[k, 0, rows, :].astype(F32), zrecv[k, 1, rows, :].astype(F32)
                x_v[0, rows, :], x_v[1, rows, :] = times(tr, ti, vr, vi)
                gr, gi = times(vr, vi, w2_v[k, 0, rows, :], w2_v[k, 1, rows, :])
                gbuf[k, 0, i, 0] = gr.astype(BF16)
                gbuf[k, 0, i, 1] = (-gi).astype(BF16)

        propagate(x_v, w3_v, tab)
        for i, rows in enumerate(blocks):
            gr, gi = times(w1_v[k, 0, rows, :], w1_v[k, 1, rows, :], w3_v[0, rows, :], w3_v[1, rows, :])
            gbuf[k, 1, i, 0] = gr.astype(BF16)
            gbuf[k, 1, i, 1] = (-gi).astype(BF16)
        for d in (4, 3, 2, 1):
            g_start(k, 1, d)

        @pl.when(z == 0)
        def _():
            for i, rows in enumerate(blocks):
                tr, ti = window(k, 1, i, row_offset)
                x_v[0, rows, :], x_v[1, rows, :] = times(tr, ti, w3_v[0, rows, :], w3_v[1, rows, :])
            propagate(x_v, w4_v, tab)
            for i, rows in enumerate(blocks):
                wr, wi = w4_v[0, rows, :], w4_v[1, rows, :]
                gr, gi = times(start_v[k, 0, rows, :], start_v[k, 1, rows, :], wr, wi)
                gbuf[k, 0, i, 0] = gr.astype(BF16)
                gbuf[k, 0, i, 1] = (-gi).astype(BF16)

        for d in (4, 3, 2, 1):
            g_start(k, 0, d)
        g_sibling(k).start()
        g_local(k).start()

        @pl.when(z == 0)
        def _():
            for i, rows in enumerate(blocks):
                tr, ti = window(k, 0, i, row_offset)
                vr, vi = times(tr, ti, w4_v[0, rows, :], w4_v[1, rows, :])
                x_v[0, rows, :], x_v[1, rows, :] = vr, -vi
            back_rows, back_cols = (SIDE - row_offset) & (SIDE - 1), (SIDE - col_offset) & (SIDE - 1)
            for ri in range(2):
                moved = roll(x_v[ri], back_rows, back_cols)
                total_v[ri] = jnp.where(k > 0, total_v[ri], 0.0) + moved

    def position(k, carry):
        first_half(k)

        @pl.when(k == 0)
        def _():
            forward_windows(1)

        @pl.when(k == 1)
        def _():
            forward_pieces(0)

        second_half(k)
        return carry

    forward_windows(0)
    lax.fori_loop(0, PER, position, 0)

    def p_copy(half):
        rows = pl.ds(pl.multiple_of((2 * half + 1 - c) * STRIP, STRIP), STRIP)
        return pltpu.make_async_remote_copy(
            src_ref=total_v.at[:, rows, :], dst_ref=part_r.at[half], send_sem=p_send.at[half],
            recv_sem=p_recv.at[half], device_id=at(q + 1 - 2 * c, j), device_id_type=MESH)

    def rs_copy(i):
        return pltpu.make_async_remote_copy(
            src_ref=rs_s.at[lax.rem(member + i, group)], dst_ref=rs_r.at[member], send_sem=rs_send.at[i],
            recv_sem=rs_recv.at[i], device_id=at(q, mate(i)), device_id_type=MESH)

    def ar_copy(half, i):
        return pltpu.make_async_remote_copy(
            src_ref=ar_s.at[half], dst_ref=ar_r.at[level], send_sem=ar_send.at[half, i],
            recv_sem=ar_recv.at[i], device_id=at(c + 2 * half, tier(i)), device_id_type=MESH)

    def ag_copy(i):
        return pltpu.make_async_remote_copy(
            src_ref=probe_out.at[member], dst_ref=probe_out.at[member], send_sem=ag_send.at[i],
            recv_sem=ag_recv.at[i], device_id=at(q, mate(i)), device_id_type=MESH)

    @pl.when(z == 0)
    def _():
        for half in range(2):
            p_copy(half).start()
        for half in range(2):
            p_copy(half).wait()
            rows = pl.ds(pl.multiple_of((2 * half + c) * STRIP, STRIP), STRIP)
            block_sum = total_v[:, rows, :] + part_r[half]
            rs_s[:, half] = block_sum.reshape(rs_s.shape[:1] + rs_s.shape[2:])
        for i in range(1, group):
            rs_copy(i).start()
        rs_r[member] = rs_s[member]

    forward_pieces(1)

    @pl.when(z == 0)
    def _():
        for i in range(1, group):
            rs_copy(i).wait_recv()
        plane_sum = rs_r[0]
        for m in range(1, group):
            plane_sum = plane_sum + rs_r[m]
        ar_s[...] = plane_sum
        ar_r[level] = plane_sum[0]
        for i in range(hi_count):
            ar_copy(1, i).start()
        for i in range(1, hi_count):
            ar_copy(0, i).start()

    @pl.when(z == 1)
    def _():
        ar_copy(1, 0).wait_recv()

    for i in range(1, hi_count):
        ar_copy(0, i).wait_recv()
    piece_sum = ar_r[0]
    for m in range(1, hi_count):
        piece_sum = piece_sum + ar_r[m]
    probe_out[member] = piece_sum
    for i in range(1, group):
        ag_copy(i).start()
    for i in range(1, group):
        ag_copy(i).wait()

    to_all.wait()
    for copy in idx_copies:
        copy.wait_send()

    @pl.when(z == 0)
    def _():
        for i in range(1, group):
            rs_copy(i).wait_send()
        for i in range(hi_count):
            ar_copy(1, i).wait_send()
        for i in range(1, hi_count):
            ar_copy(0, i).wait_send()

    def drain(k, carry):
        z_copy(k).wait_send()
        t_sibling(k).wait_send()
        g_sibling(k).wait_send()
        g_local(k).wait()
        g_arrival(k, 1 - c, RIM * (1 - c)).wait_recv()

        def act(arrival, onward):
            onward.wait_send()

        t_forward(k, act)
        g_forward(k, act)
        for e in range(1, RIM + 1):
            for b in range(2):
                d = strip_of(b, e)
                t_copy(k, d, b, region(e)).wait_send()
                g_copy(k, b, e, region(e)).wait_send()
                g_arrival(k, b, d).wait_recv()

        @pl.when((z == 1) & (c == 1))
        def _():
            x_copy(k).wait_send()

        return carry

    lax.fori_loop(0, PER, drain, 0)


def main_call(transmission, probe, exit_adjoint, scan_row, scan_col):
    n_scan = lax.axis_size("scan")
    across = 4 if n_scan == 64 else 2
    group = RIM * across
    hi_count = n_scan // group
    piece = (16 // group, 8, SIDE)
    hbm_spec = pl.BlockSpec(memory_space=pltpu.HBM)
    vmem_spec = pl.BlockSpec(memory_space=pltpu.VMEM)
    field = (2, SIDE, SIDE)
    dma = pltpu.SemaphoreType.DMA
    columns = transmission.shape[3]
    return pl.pallas_call(
        functools.partial(main_kernel, across, hi_count, n_scan),
        out_shape=(
            jax.ShapeDtypeStruct((PER, 2, RIM + 1, 2, STRIP, SIDE), BF16),
            jax.ShapeDtypeStruct((RIM + 1, 8, 128), jnp.int32),
            jax.ShapeDtypeStruct((group,) + piece, F32),
        ),
        in_specs=[hbm_spec] * 4 + [pl.BlockSpec(memory_space=pltpu.SMEM)] * 2,
        out_specs=(hbm_spec, hbm_spec, vmem_spec),
        scratch_shapes=[
            pltpu.VMEM((columns // HALF, 2, STRIP, HALF), F32),
            pltpu.VMEM((2, 2, 2, SIDE, SIDE), BF16),
            pltpu.VMEM(field, F32),
            pltpu.VMEM((PER,) + field, F32),
            pltpu.VMEM((8, 128), jnp.int32),
            pltpu.VMEM((RIM + 1, 8, 128), jnp.int32),
            pltpu.SMEM((RIM + 1, 8, 128), jnp.int32),
            pltpu.VMEM((PER,) + field, BF16),
            pltpu.VMEM((PER,) + field, BF16),
            pltpu.VMEM((PER, RIM + 1, 2, 2, STRIP, SIDE), BF16),
            pltpu.VMEM((PER, 2, RIM + 1, 2, STRIP, SIDE), BF16),
            pltpu.VMEM(field, F32),
            pltpu.VMEM((PER,) + field, F32),
            pltpu.VMEM((PER,) + field, F32),
            pltpu.VMEM((PER,) + field, F32),
            pltpu.VMEM(field, F32),
            pltpu.VMEM(field, F32),
            pltpu.VMEM((PER,) + field, BF16),
            pltpu.VMEM((PER,) + field, BF16),
            pltpu.VMEM((PER, RIM + 1, 2, STRIP, SIDE), BF16),
            pltpu.VMEM((PER, RIM + 1, 2, STRIP, SIDE), BF16),
            pltpu.VMEM((PER, 2, RIM, 2, STRIP, SIDE), BF16),
            pltpu.VMEM(field, F32),
            pltpu.VMEM((2, 2, STRIP, SIDE), F32),
            pltpu.VMEM((group, 2) + piece, F32),
            pltpu.VMEM((group, 2) + piece, F32),
            pltpu.VMEM((2,) + piece, F32),
            pltpu.VMEM((hi_count,) + piece, F32),
            dma((6,)),
            dma((columns // HALF,)),
            dma((PER,)),
            dma((PER,)),
            dma((RIM + 1,)),
            dma((RIM + 1,)),
            dma((PER, RIM + 1, 2)),
            dma((PER, 2, RIM + 1)),
            dma((PER, RIM + 1)),
            dma((PER, RIM + 1)),
            dma((PER,)),
            dma((PER,)),
            dma((PER, 2, RIM + 1)),
            dma((PER, 2, RIM + 1)),
            dma((PER, RIM + 1)),
            dma((PER, RIM + 1)),
            dma((2,)),
            dma((2,)),
            dma((group,)),
            dma((group,)),
            dma((2, hi_count)),
            dma((hi_count,)),
            dma((group,)),
            dma((group,)),
        ],
        compiler_params=pltpu.CompilerParams(
            collective_id=0, has_side_effects=True, vmem_limit_bytes=62 * 1024 * 1024
        ),
        cost_estimate=pl.CostEstimate(flops=8 * 12 * 2 * SIDE**3, bytes_accessed=8 << 20, transcendentals=0),
        name="waves",
    )(transmission, probe, exit_adjoint, jnp.asarray(tables()), scan_row, scan_col)


def deposit_kernel(idx, pieces, probe_in, grad, probe_out):
    probe_out[...] = probe_in[...]
    grad[...] = jnp.zeros_like(grad)
    lane = lax.broadcasted_iota(jnp.int32, (1, 1, HALF), 2)
    row = lax.broadcasted_iota(jnp.int32, (1, STRIP, 1), 1)

    def add(n, carry):
        d = n // 4
        core = (n // 2) % 2
        k = n % 2
        row_offset = idx[d, core, k] & (STRIP - 1)
        col = idx[d, 2 + core, k]
        block = lax.shift_right_logical(col, 7)
        col_offset = col & (HALF - 1)
        low = jnp.where(d == 0, row_offset, 0)
        high = jnp.where(d == RIM, row_offset, STRIP)
        keep = (row >= low) & (row < high)
        piece = jnp.where(keep, pieces[k, core, d].astype(F32), 0.0)
        first, second = piece[:, :, :HALF], piece[:, :, HALF:]
        here = lane >= col_offset
        third_block = jnp.minimum(block + 2, grad.shape[3] // HALF - 1)
        for where_to, value in (
            (block, jnp.where(here, first, 0.0)),
            (block + 1, second),
            (third_block, jnp.where(here, 0.0, first)),
        ):
            cols = pl.ds(pl.multiple_of(where_to * HALF, HALF), HALF)
            grad[0, :, :, cols] = grad[0, :, :, cols] + value
        return carry

    lax.fori_loop(0, 4 * (RIM + 1), add, 0)


def deposit_call(idx_all, pieces, probe_sum, columns):
    vmem_spec = pl.BlockSpec(memory_space=pltpu.VMEM)
    return pl.pallas_call(
        deposit_kernel,
        out_shape=(
            jax.ShapeDtypeStruct((1, 2, STRIP, columns), F32),
            jax.ShapeDtypeStruct(probe_sum.shape, F32),
        ),
        in_specs=[pl.BlockSpec(memory_space=pltpu.SMEM), vmem_spec, vmem_spec],
        out_specs=(vmem_spec, vmem_spec),
        compiler_params=pltpu.CompilerParams(vmem_limit_bytes=62 * 1024 * 1024),
        name="deposit",
    )(idx_all, pieces, probe_sum)


def local(transmission, probe, exit_adjoint, scan_row, scan_col):
    pieces, idx_all, probe_sum = main_call(transmission, probe, exit_adjoint, scan_row, scan_col)
    object_grad, probe_grad = deposit_call(idx_all, pieces, probe_sum, transmission.shape[3])
    return object_grad, probe_grad.reshape(2, STRIP, SIDE)


def solution(mesh):
    placed = (
        P("depth", None, "scan", None),
        P(),
        P(None, "scan", None, None, None),
        P(None, "scan"),
        P(None, "scan"),
    )
    return jax.shard_map(
        local,
        mesh=mesh,
        in_specs=placed,
        out_specs=(P("depth", None, "scan", None), P(None, "depth", None)),
        check_vma=False,
    )
```

```python
import functools
import math

import jax
import jax.numpy as jnp
import numpy as np
from jax import lax
from jax.experimental import pallas as pl
from jax.experimental.pallas import tpu as pltpu
from jax.sharding import PartitionSpec as P

FRESNEL = 0.25
SIDE = 256
HALF = SIDE // 2
STRIP = 64
RIM = SIDE // STRIP
BATCHES = 2
PER = 2
F32 = jnp.float32
BF16 = jnp.bfloat16
MESH = pl.DeviceIdType.MESH


def tables():
    k = np.arange(SIDE)
    f = np.where(k < HALF, k, k - SIDE).astype(np.float64)
    h = np.exp(-1j * math.pi * FRESNEL * f * f / SIDE)
    dft = np.exp(-2j * math.pi * (np.outer(k, k) % SIDE) / SIDE)
    a = (dft.conj() / SIDE) @ (h[:, None] * dft)
    lefts, rights = [], []
    for sign in (1.0, -1.0):
        m = (a[:HALF, :HALF] + sign * a[:HALF, HALF:]) / 2.0
        left = np.block([[m.real, -m.imag], [m.imag, m.real]]).astype(np.float32)
        for out, full in ((lefts, left), (rights, left.T.copy())):
            high = full.astype(jnp.bfloat16)
            low = (full - high.astype(np.float32)).astype(jnp.bfloat16)
            out.append(np.stack([high, low]))
    return np.stack([np.stack(lefts), np.stack(rights)])


def dot(a, b):
    return jnp.dot(a, b, preferred_element_type=F32)


def split(x):
    high = x.astype(BF16)
    return high, (x - high.astype(F32)).astype(BF16)


def propagate(x_ref, w_ref, tab):
    middle = []
    for a in range(2):
        parts = []
        for ri in range(2):
            top, low = x_ref[ri, :HALF, :], x_ref[ri, HALF:, :]
            v = top + low if a == 0 else top - low
            l, r = v[:, :HALF], v[:, HALF:]
            parts.append(jnp.concatenate([l + r, l - r], axis=1))
        high, low = split(jnp.concatenate(parts, axis=0))
        left_high, left_low = tab[0, a, 0], tab[0, a, 1]
        middle.append(dot(left_high, high) + dot(left_low, high) + dot(left_high, low))
    sectors = []
    for b in range(2):
        cols = slice(b * HALF, (b + 1) * HALF)
        rows = [jnp.concatenate([z[:HALF, cols], z[HALF:, cols]], axis=1) for z in middle]
        high, low = split(jnp.concatenate(rows, axis=0))
        right_high, right_low = tab[1, b, 0], tab[1, b, 1]
        sectors.append(dot(high, right_high) + dot(high, right_low) + dot(low, right_high))
    for ri in range(2):
        cols = slice(ri * HALF, (ri + 1) * HALF)
        for half_col in range(2):
            s, d = sectors[0][:, cols], sectors[1][:, cols]
            v = s + d if half_col == 0 else s - d
            out = slice(half_col * HALF, (half_col + 1) * HALF)
            w_ref[ri, :HALF, out] = v[:HALF] + v[HALF:]
            w_ref[ri, HALF:, out] = v[:HALF] - v[HALF:]


def times(ar, ai, br, bi):
    return ar * br - ai * bi, ar * bi + ai * br


def main_kernel(
    across, hi_count, n_scan,
    trans, probe, exit_adjoint, table_in, row_in, col_in,
    pieces, idx_all, probe_out,
    strip, tab, probe_v, exit_v, idx_in, idx_v, idx_s,
    xsend, xrecv, sbuf, tbuf, x_v, start_v, w1_v, w2_v, w3_v, w4_v, zsend, zrecv,
    t_transit, g_transit, gbuf, total_v, part_r, rs_s, rs_r, ar_s, ar_r,
    local_sems, strip_sems, x_send, x_recv, idx_send, idx_recv, t_send, t_recv, tt_send, tt_recv, z_send, z_recv,
    g_send, g_recv, gt_send, gt_recv, p_send, p_recv, rs_send, rs_recv, ar_send, ar_recv, ag_send, ag_recv,
):
    q = lax.axis_index("depth")
    j = lax.axis_index("scan")
    z = q // 2
    c = q % 2
    group = RIM * across
    member = j % group
    level = j // group
    y = j % RIM
    x = member // RIM
    span = RIM * (across - 1)

    def at(depth, scan):
        return {"depth": depth, "scan": scan}

    def region(step):
        return lax.rem(j + step + n_scan, n_scan)

    def strip_of(core, e):
        return e + core * (RIM - 2 * e)

    def both(sign, plus, minus):
        return ((sign > 0) & plus) | ((sign < 0) & minus)

    def turns(sign, e):
        return both(sign, y + e >= RIM, y < e)

    def turned_here(sign, e):
        return both(sign, y < e, y >= RIM - e)

    def leaves(sign):
        return both(sign, x == across - 1, x == 0)

    def left_here(sign):
        return both(sign, x == 0, x == across - 1)

    def mate(i):
        return level * group + lax.rem(member + i, group)

    def tier(i):
        return lax.rem(level + i, hi_count) * group + member

    loads = [
        pltpu.make_async_copy(table_in, tab, local_sems.at[1]),
        pltpu.make_async_copy(probe, probe_v, local_sems.at[2]),
        pltpu.make_async_copy(exit_adjoint.at[c], exit_v, local_sems.at[3]),
    ]

    def strip_copy(i):
        cols = pl.ds(pl.multiple_of(i * HALF, HALF), HALF)
        return pltpu.make_async_copy(trans.at[0, :, :, cols], strip.at[i], strip_sems.at[i])

    for copy in loads:
        copy.start()

    def start_strip(i, carry):
        strip_copy(i).start()
        return carry

    def wait_strip(i, carry):
        strip_copy(i).wait()
        return carry

    lax.fori_loop(0, strip.shape[0], start_strip, 0)

    at_row = lax.broadcasted_iota(jnp.int32, (8, 128), 0)
    at_lane = lax.broadcasted_iota(jnp.int32, (8, 128), 1)
    own = jnp.zeros((8, 128), jnp.int32)
    for b in range(BATCHES):
        for k in range(PER):
            own = jnp.where((at_row == b) & (at_lane == k), row_in[b, k], own)
            own = jnp.where((at_row == 2 + b) & (at_lane == k), col_in[b, k], own)
    idx_in[...] = own
    idx_v[0] = own

    barrier = pltpu.get_barrier_semaphore()
    partners = [at(q + 1 - 2 * c, j), at(q + 2 - 4 * z, j)]
    for d in range(1, RIM + 1):
        for b in range(2):
            partners.append(at(2 * z + b, region(d)))
            partners.append(at(2 * z + b, region(-d)))
    for i in range(1, group):
        partners.append(at(q, mate(i)))
    for i in range(1, hi_count):
        partners.append(at(q, tier(i)))
        partners.append(at(q + 2 - 4 * z, tier(i)))
    for device in partners:
        pl.semaphore_signal(barrier, inc=1, device_id=device, device_id_type=MESH)
    crossing = ((x == 0, span), (x == across - 1, -span))
    for edge, step in crossing:
        @pl.when(edge)
        def _(step=step):
            pl.semaphore_signal(
                barrier, inc=1, device_id=at(q + 1 - 2 * c, region(step)), device_id_type=MESH)
    on_edge = ((x == 0) | (x == across - 1)).astype(jnp.int32)
    pl.semaphore_wait(barrier, len(partners) + on_edge)

    def x_copy(k):
        return pltpu.make_async_remote_copy(
            src_ref=xsend.at[k], dst_ref=xrecv.at[k], send_sem=x_send.at[k], recv_sem=x_recv.at[k],
            device_id=at(q, region(RIM)), device_id_type=MESH)

    idx_copies = [
        pltpu.make_async_remote_copy(
            src_ref=idx_in, dst_ref=idx_v.at[d], send_sem=idx_send.at[d], recv_sem=idx_recv.at[d],
            device_id=at(q, region(d)), device_id_type=MESH)
        for d in range(1, RIM + 1)
    ]
    for copy in idx_copies:
        copy.start()

    loads[2].wait()

    @pl.when((z == 1) & (c == 1))
    def _():
        for k in range(PER):
            xsend[k] = exit_v[k].astype(BF16)
        x_copy(0).start()

    for copy in idx_copies:
        copy.wait_recv()
    to_smem = pltpu.make_async_copy(idx_v, idx_s, local_sems.at[5])
    to_smem.start()
    to_all = pltpu.make_async_copy(idx_v, idx_all, local_sems.at[4])
    to_all.start()
    to_smem.wait()
    lax.fori_loop(0, strip.shape[0], wait_strip, 0)

    lane = lax.broadcasted_iota(jnp.int32, (1, 1, HALF), 2)
    last_block = strip.shape[0] - 1

    def t_copy(k, d, b, target, entry=None):
        return pltpu.make_async_remote_copy(
            src_ref=sbuf.at[k, d, b],
            dst_ref=tbuf.at[k, c, d] if entry is None else t_transit.at[k, entry],
            send_sem=t_send.at[k, d, b],
            recv_sem=t_recv.at[k, c, d] if entry is None else tt_recv.at[k, entry],
            device_id=at(2 * z + b, target), device_id_type=MESH)

    def t_start(k, e, b):
        d, sign = strip_of(b, e), 2 * b - 1
        if e == RIM:
            detour, step, entry = leaves(sign), -sign * span, e - 1 + c
        else:
            detour, step, entry = turns(sign, e) & (c == b), -sign * (RIM - e), e - 1

        @pl.when(detour)
        def _():
            t_copy(k, d, b, region(step), entry).start()

        @pl.when(jnp.logical_not(detour))
        def _():
            t_copy(k, d, b, region(sign * e)).start()

    def t_onward(k, slot, e, entry, step):
        d = strip_of(c, e)
        return pltpu.make_async_remote_copy(
            src_ref=t_transit.at[k, entry], dst_ref=tbuf.at[k, slot, d],
            send_sem=tt_send.at[k, entry], recv_sem=t_recv.at[k, slot, d],
            device_id=at(q, region(step)), device_id_type=MESH)

    def t_transit_arrival(k, entry):
        return pltpu.make_async_remote_copy(
            src_ref=sbuf.at[k, 0, 0], dst_ref=t_transit.at[k, entry],
            send_sem=tt_send.at[k, entry], recv_sem=tt_recv.at[k, entry],
            device_id=at(q + 1 - 2 * c, j), device_id_type=MESH)

    def t_forward(k, act):
        sign = 2 * c - 1

        for e in range(1, RIM):
            @pl.when(turned_here(sign, e))
            def _(e=e):
                act(t_transit_arrival(k, e - 1), t_onward(k, c, e, e - 1, sign * RIM))

        @pl.when(left_here(sign))
        def _():
            for slot in range(2):
                entry = RIM - 1 + slot
                act(t_transit_arrival(k, entry), t_onward(k, slot, RIM, entry, sign * RIM * across))

    def t_sibling(k):
        d = RIM * (1 - c)
        return pltpu.make_async_remote_copy(
            src_ref=sbuf.at[k, d, 1 - c], dst_ref=tbuf.at[k, c, d],
            send_sem=t_send.at[k, d, 1 - c], recv_sem=t_recv.at[k, c, d],
            device_id=at(q + 1 - 2 * c, j), device_id_type=MESH)

    def t_local(k):
        d = RIM * c
        return pltpu.make_async_copy(sbuf.at[k, d, c], tbuf.at[k, c, d], t_send.at[k, d, c])

    def t_arrival(k, slot, d):
        return pltpu.make_async_remote_copy(
            src_ref=sbuf.at[k, 0, 0], dst_ref=tbuf.at[k, slot, d],
            send_sem=t_send.at[k, d, 0], recv_sem=t_recv.at[k, slot, d],
            device_id=at(q + 1 - 2 * c, j), device_id_type=MESH)

    def send_windows(k):
        for e in (4, 3, 2, 1, 0):
            for b in range(2):
                d = strip_of(b, e)
                col = idx_s[d, 2 + b, k]
                block = lax.shift_right_logical(col, 7)
                offset = col & (HALF - 1)
                first, second = strip[block], strip[block + 1]
                third = strip[jnp.minimum(block + 2, last_block)]
                sbuf[k, d, b, :, :, :HALF] = jnp.where(lane >= offset, first, third).astype(BF16)
                sbuf[k, d, b, :, :, HALF:] = second.astype(BF16)
                if e > 0:
                    t_start(k, e, b)
        t_sibling(k).start()
        t_local(k).start()

    send_windows(0)

    @pl.when((z == 1) & (c == 1))
    def _():
        x_copy(1).start()


    def wait_windows(k):
        t_local(k).wait()
        t_arrival(k, 1 - c, RIM * c).wait_recv()
        for e in range(1, RIM + 1):
            for slot in range(2):
                t_arrival(k, slot, strip_of(c, e)).wait_recv()

    row = lax.broadcasted_iota(jnp.int32, (STRIP, 1), 0)

    def offsets(k):
        return idx_s[RIM * c, c, k] & (STRIP - 1), idx_s[RIM * c, 2 + c, k] & (HALF - 1)

    def window(k, slot, block, row_offset):
        if block > 0:
            return tbuf[k, slot, block, 0].astype(F32), tbuf[k, slot, block, 1].astype(F32)
        here = row >= row_offset
        return tuple(
            jnp.where(here, tbuf[k, slot, 0, ri].astype(F32), tbuf[k, slot, RIM, ri].astype(F32))
            for ri in range(2)
        )

    blocks = [slice(i * STRIP, (i + 1) * STRIP) for i in range(RIM)]

    def roll(x, rows, cols):
        return pltpu.roll(pltpu.roll(x, rows, 0), cols, 1)

    def z_copy(k):
        return pltpu.make_async_remote_copy(
            src_ref=zsend.at[k], dst_ref=zrecv.at[k], send_sem=z_send.at[k], recv_sem=z_recv.at[k],
            device_id=at(q + 2 - 4 * z, j), device_id_type=MESH)

    for copy in loads[:2]:
        copy.wait()

    def send_later(k):
        @pl.when(k == 0)
        def _():
            send_windows(1)

    def first_half(k):
        row_offset, col_offset = offsets(k)

        @pl.when(z == 0)
        def _():
            for ri in range(2):
                start_v[k, ri] = roll(probe_v[ri], row_offset, col_offset)
            wait_windows(k)
            send_later(k)
            for i, rows in enumerate(blocks):
                tr, ti = window(k, 0, i, row_offset)
                x_v[0, rows, :], x_v[1, rows, :] = times(tr, ti, start_v[k, 0, rows, :], start_v[k, 1, rows, :])

        @pl.when(z == 1)
        def _():
            @pl.when(c == 0)
            def _():
                x_v[...] = exit_v[k]

            @pl.when(c == 1)
            def _():
                x_copy(k).wait_recv()
                x_v[...] = xrecv[k].astype(F32)

            x_v[0] = roll(x_v[0], row_offset, col_offset)
            x_v[1] = -roll(x_v[1], row_offset, col_offset)

        propagate(x_v, w1_v.at[k], tab)

        @pl.when(z == 1)
        def _():
            wait_windows(k)
            send_later(k)

        for i, rows in enumerate(blocks):
            tr, ti = window(k, 1, i, row_offset)
            x_v[0, rows, :], x_v[1, rows, :] = times(tr, ti, w1_v[k, 0, rows, :], w1_v[k, 1, rows, :])
        propagate(x_v, w2_v.at[k], tab)

        @pl.when(z == 0)
        def _():
            zsend[k] = w2_v[k].astype(BF16)

        @pl.when(z == 1)
        def _():
            for i, rows in enumerate(blocks):
                tr, ti = window(k, 0, i, row_offset)
                vr, vi = times(tr, ti, w2_v[k, 0, rows, :], w2_v[k, 1, rows, :])
                zsend[k, 0, rows, :] = vr.astype(BF16)
                zsend[k, 1, rows, :] = vi.astype(BF16)

        z_copy(k).start()

    def forward_windows(k):
        def act(arrival, onward):
            arrival.wait_recv()
            onward.start()
        t_forward(k, act)


    def g_copy(k, slot, e, target, entry=None):
        d = strip_of(c, e)
        return pltpu.make_async_remote_copy(
            src_ref=gbuf.at[k, slot, lax.rem(d, RIM)],
            dst_ref=pieces.at[k, c, d] if entry is None else g_transit.at[k, entry],
            send_sem=g_send.at[k, slot, e],
            recv_sem=g_recv.at[k, c, d] if entry is None else gt_recv.at[k, entry],
            device_id=at(2 * z + slot, target), device_id_type=MESH)

    def g_start(k, slot, e):
        sign = 1 - 2 * c
        if e == RIM:
            detour, step, entry = leaves(sign), -sign * span, e - 1 + c
        else:
            detour, step, entry = turns(sign, e) & (c == slot), -sign * (RIM - e), e - 1

        @pl.when(detour)
        def _():
            g_copy(k, slot, e, region(step), entry).start()

        @pl.when(jnp.logical_not(detour))
        def _():
            g_copy(k, slot, e, region(sign * e)).start()

    def g_onward(k, core, d, entry, step):
        return pltpu.make_async_remote_copy(
            src_ref=g_transit.at[k, entry], dst_ref=pieces.at[k, core, d],
            send_sem=gt_send.at[k, entry], recv_sem=g_recv.at[k, core, d],
            device_id=at(q, region(step)), device_id_type=MESH)

    def g_transit_arrival(k, entry):
        return pltpu.make_async_remote_copy(
            src_ref=gbuf.at[k, 0, 0], dst_ref=g_transit.at[k, entry],
            send_sem=gt_send.at[k, entry], recv_sem=gt_recv.at[k, entry],
            device_id=at(q + 1 - 2 * c, j), device_id_type=MESH)

    def g_forward(k, act):
        for core in range(2):
            @pl.when(left_here(1 - 2 * core))
            def _(core=core):
                entry, step = RIM - 1 + core, (1 - 2 * core) * RIM * across
                act(g_transit_arrival(k, entry), g_onward(k, core, strip_of(core, RIM), entry, step))

        sign = 1 - 2 * c
        for e in range(1, RIM):
            @pl.when(turned_here(sign, e))
            def _(e=e):
                act(g_transit_arrival(k, e - 1), g_onward(k, c, strip_of(c, e), e - 1, sign * RIM))

    def forward_pieces(k):
        def act(arrival, onward):
            arrival.wait_recv()
            onward.start()
        g_forward(k, act)

    def g_sibling(k):
        return pltpu.make_async_remote_copy(
            src_ref=gbuf.at[k, 1 - c, 0], dst_ref=pieces.at[k, c, RIM * c],
            send_sem=g_send.at[k, 1, 0], recv_sem=g_recv.at[k, c, RIM * c],
            device_id=at(q + 1 - 2 * c, j), device_id_type=MESH)

    def g_local(k):
        return pltpu.make_async_copy(gbuf.at[k, c, 0], pieces.at[k, c, RIM * c], g_send.at[k, 0, 0])

    def g_arrival(k, core, d):
        return pltpu.make_async_remote_copy(
            src_ref=gbuf.at[k, 0, 0], dst_ref=pieces.at[k, core, d],
            send_sem=g_send.at[k, 0, d], recv_sem=g_recv.at[k, core, d],
            device_id=at(q + 1 - 2 * c, j), device_id_type=MESH)

    def second_half(k):
        row_offset, col_offset = offsets(k)
        z_copy(k).wait_recv()

        @pl.when(z == 0)
        def _():
            x_v[...] = zrecv[k].astype(F32)

        @pl.when(z == 1)
        def _():
            for i, rows in enumerate(blocks):
                tr, ti = window(k, 0, i, row_offset)
                vr, vi = zrecv[k, 0, rows, :].astype(F32), zrecv[k, 1, rows, :].astype(F32)
                x_v[0, rows, :], x_v[1, rows, :] = times(tr, ti, vr, vi)
                gr, gi = times(vr, vi, w2_v[k, 0, rows, :], w2_v[k, 1, rows, :])
                gbuf[k, 0, i, 0] = gr.astype(BF16)
                gbuf[k, 0, i, 1] = (-gi).astype(BF16)

        propagate(x_v, w3_v, tab)
        for i, rows in enumerate(blocks):
            gr, gi = times(w1_v[k, 0, rows, :], w1_v[k, 1, rows, :], w3_v[0, rows, :], w3_v[1, rows, :])
            gbuf[k, 1, i, 0] = gr.astype(BF16)
            gbuf[k, 1, i, 1] = (-gi).astype(BF16)
        for d in (4, 3, 2, 1):
            g_start(k, 1, d)

        @pl.when(z == 0)
        def _():
            for i, rows in enumerate(blocks):
                tr, ti = window(k, 1, i, row_offset)
                x_v[0, rows, :], x_v[1, rows, :] = times(tr, ti, w3_v[0, rows, :], w3_v[1, rows, :])
            propagate(x_v, w4_v, tab)
            for i, rows in enumerate(blocks):
                wr, wi = w4_v[0, rows, :], w4_v[1, rows, :]
                gr, gi = times(start_v[k, 0, rows, :], start_v[k, 1, rows, :], wr, wi)
                gbuf[k, 0, i, 0] = gr.astype(BF16)
                gbuf[k, 0, i, 1] = (-gi).astype(BF16)

        for d in (4, 3, 2, 1):
            g_start(k, 0, d)
        g_sibling(k).start()
        g_local(k).start()

        @pl.when(z == 0)
        def _():
            for i, rows in enumerate(blocks):
                tr, ti = window(k, 0, i, row_offset)
                vr, vi = times(tr, ti, w4_v[0, rows, :], w4_v[1, rows, :])
                x_v[0, rows, :], x_v[1, rows, :] = vr, -vi
            back_rows, back_cols = (SIDE - row_offset) & (SIDE - 1), (SIDE - col_offset) & (SIDE - 1)
            for ri in range(2):
                moved = roll(x_v[ri], back_rows, back_cols)
                total_v[ri] = jnp.where(k > 0, total_v[ri], 0.0) + moved

    def position(k, carry):
        first_half(k)

        @pl.when(k == 0)
        def _():
            forward_windows(1)

        @pl.when(k == 1)
        def _():
            forward_pieces(0)

        second_half(k)
        return carry

    forward_windows(0)
    lax.fori_loop(0, PER, position, 0)

    def p_copy(half):
        rows = pl.ds(pl.multiple_of((2 * half + 1 - c) * STRIP, STRIP), STRIP)
        return pltpu.make_async_remote_copy(
            src_ref=total_v.at[:, rows, :], dst_ref=part_r.at[half], send_sem=p_send.at[half],
            recv_sem=p_recv.at[half], device_id=at(q + 1 - 2 * c, j), device_id_type=MESH)

    def rs_copy(i):
        return pltpu.make_async_remote_copy(
            src_ref=rs_s.at[lax.rem(member + i, group)], dst_ref=rs_r.at[member], send_sem=rs_send.at[i],
            recv_sem=rs_recv.at[i], device_id=at(q, mate(i)), device_id_type=MESH)

    def ar_copy(half, i):
        return pltpu.make_async_remote_copy(
            src_ref=ar_s.at[half], dst_ref=ar_r.at[level], send_sem=ar_send.at[half, i],
            recv_sem=ar_recv.at[i], device_id=at(c + 2 * half, tier(i)), device_id_type=MESH)

    def ag_copy(i):
        return pltpu.make_async_remote_copy(
            src_ref=probe_out.at[member], dst_ref=probe_out.at[member], send_sem=ag_send.at[i],
            recv_sem=ag_recv.at[i], device_id=at(q, mate(i)), device_id_type=MESH)

    @pl.when(z == 0)
    def _():
        for half in range(2):
            p_copy(half).start()
        halves = []
        for half in range(2):
            p_copy(half).wait()
            rows = pl.ds(pl.multiple_of((2 * half + c) * STRIP, STRIP), STRIP)
            block_sum = total_v[:, rows, :] + part_r[half]
            halves.append(block_sum.reshape(group, rs_s.shape[1] // 2, SIDE))
        rs_s[...] = jnp.concatenate(halves, axis=1).astype(BF16)
        for i in range(1, group):
            rs_copy(i).start()
        rs_r[member] = rs_s[member]

    forward_pieces(1)

    @pl.when(z == 0)
    def _():
        for i in range(1, group):
            rs_copy(i).wait_recv()
        plane_sum = rs_r[0].astype(F32)
        for m in range(1, group):
            plane_sum = plane_sum + rs_r[m].astype(F32)
        plane_sum = plane_sum.reshape(ar_s.shape)
        ar_s[...] = plane_sum
        ar_r[level] = plane_sum[0]
        for i in range(hi_count):
            ar_copy(1, i).start()
        for i in range(1, hi_count):
            ar_copy(0, i).start()

    @pl.when(z == 1)
    def _():
        ar_copy(1, 0).wait_recv()

    for i in range(1, hi_count):
        ar_copy(0, i).wait_recv()
    piece_sum = ar_r[0]
    for m in range(1, hi_count):
        piece_sum = piece_sum + ar_r[m]
    probe_out[member] = piece_sum
    for i in range(1, group):
        ag_copy(i).start()
    for i in range(1, group):
        ag_copy(i).wait()

    to_all.wait()
    for copy in idx_copies:
        copy.wait_send()

    @pl.when(z == 0)
    def _():
        for i in range(1, group):
            rs_copy(i).wait_send()
        for i in range(hi_count):
            ar_copy(1, i).wait_send()
        for i in range(1, hi_count):
            ar_copy(0, i).wait_send()

    def drain(k, carry):
        z_copy(k).wait_send()
        t_sibling(k).wait_send()
        g_sibling(k).wait_send()
        g_local(k).wait()
        g_arrival(k, 1 - c, RIM * (1 - c)).wait_recv()

        def act(arrival, onward):
            onward.wait_send()

        t_forward(k, act)
        g_forward(k, act)
        for e in range(1, RIM + 1):
            for b in range(2):
                d = strip_of(b, e)
                t_copy(k, d, b, region(e)).wait_send()
                g_copy(k, b, e, region(e)).wait_send()
                g_arrival(k, b, d).wait_recv()

        @pl.when((z == 1) & (c == 1))
        def _():
            x_copy(k).wait_send()

        return carry

    lax.fori_loop(0, PER, drain, 0)


def main_call(transmission, probe, exit_adjoint, scan_row, scan_col):
    n_scan = lax.axis_size("scan")
    across = 4 if n_scan == 64 else 2
    group = RIM * across
    hi_count = n_scan // group
    piece = (16 // group, 8, SIDE)
    hbm_spec = pl.BlockSpec(memory_space=pltpu.HBM)
    vmem_spec = pl.BlockSpec(memory_space=pltpu.VMEM)
    field = (2, SIDE, SIDE)
    dma = pltpu.SemaphoreType.DMA
    columns = transmission.shape[3]
    return pl.pallas_call(
        functools.partial(main_kernel, across, hi_count, n_scan),
        out_shape=(
            jax.ShapeDtypeStruct((PER, 2, RIM + 1, 2, STRIP, SIDE), BF16),
            jax.ShapeDtypeStruct((RIM + 1, 8, 128), jnp.int32),
            jax.ShapeDtypeStruct((group,) + piece, F32),
        ),
        in_specs=[hbm_spec] * 4 + [pl.BlockSpec(memory_space=pltpu.SMEM)] * 2,
        out_specs=(hbm_spec, hbm_spec, vmem_spec),
        scratch_shapes=[
            pltpu.VMEM((columns // HALF, 2, STRIP, HALF), F32),
            pltpu.VMEM((2, 2, 2, SIDE, SIDE), BF16),
            pltpu.VMEM(field, F32),
            pltpu.VMEM((PER,) + field, F32),
            pltpu.VMEM((8, 128), jnp.int32),
            pltpu.VMEM((RIM + 1, 8, 128), jnp.int32),
            pltpu.SMEM((RIM + 1, 8, 128), jnp.int32),
            pltpu.VMEM((PER,) + field, BF16),
            pltpu.VMEM((PER,) + field, BF16),
            pltpu.VMEM((PER, RIM + 1, 2, 2, STRIP, SIDE), BF16),
            pltpu.VMEM((PER, 2, RIM + 1, 2, STRIP, SIDE), BF16),
            pltpu.VMEM(field, F32),
            pltpu.VMEM((PER,) + field, F32),
            pltpu.VMEM((PER,) + field, F32),
            pltpu.VMEM((PER,) + field, F32),
            pltpu.VMEM(field, F32),
            pltpu.VMEM(field, F32),
            pltpu.VMEM((PER,) + field, BF16),
            pltpu.VMEM((PER,) + field, BF16),
            pltpu.VMEM((PER, RIM + 1, 2, STRIP, SIDE), BF16),
            pltpu.VMEM((PER, RIM + 1, 2, STRIP, SIDE), BF16),
            pltpu.VMEM((PER, 2, RIM, 2, STRIP, SIDE), BF16),
            pltpu.VMEM(field, F32),
            pltpu.VMEM((2, 2, STRIP, SIDE), F32),
            pltpu.VMEM((group, 16 * piece[0], SIDE), BF16),
            pltpu.VMEM((group, 16 * piece[0], SIDE), BF16),
            pltpu.VMEM((2,) + piece, F32),
            pltpu.VMEM((hi_count,) + piece, F32),
            dma((6,)),
            dma((columns // HALF,)),
            dma((PER,)),
            dma((PER,)),
            dma((RIM + 1,)),
            dma((RIM + 1,)),
            dma((PER, RIM + 1, 2)),
            dma((PER, 2, RIM + 1)),
            dma((PER, RIM + 1)),
            dma((PER, RIM + 1)),
            dma((PER,)),
            dma((PER,)),
            dma((PER, 2, RIM + 1)),
            dma((PER, 2, RIM + 1)),
            dma((PER, RIM + 1)),
            dma((PER, RIM + 1)),
            dma((2,)),
            dma((2,)),
            dma((group,)),
            dma((group,)),
            dma((2, hi_count)),
            dma((hi_count,)),
            dma((group,)),
            dma((group,)),
        ],
        compiler_params=pltpu.CompilerParams(
            collective_id=0, has_side_effects=True, vmem_limit_bytes=62 * 1024 * 1024
        ),
        cost_estimate=pl.CostEstimate(flops=8 * 12 * 2 * SIDE**3, bytes_accessed=8 << 20, transcendentals=0),
        name="waves",
    )(transmission, probe, exit_adjoint, jnp.asarray(tables()), scan_row, scan_col)


def deposit_kernel(idx, pieces, probe_in, grad, probe_out):
    probe_out[...] = probe_in[...]
    grad[...] = jnp.zeros_like(grad)
    lane = lax.broadcasted_iota(jnp.int32, (1, 1, HALF), 2)
    row = lax.broadcasted_iota(jnp.int32, (1, STRIP, 1), 1)

    def add(n, carry):
        d = n // 4
        core = (n // 2) % 2
        k = n % 2
        row_offset = idx[d, core, k] & (STRIP - 1)
        col = idx[d, 2 + core, k]
        block = lax.shift_right_logical(col, 7)
        col_offset = col & (HALF - 1)
        low = jnp.where(d == 0, row_offset, 0)
        high = jnp.where(d == RIM, row_offset, STRIP)
        keep = (row >= low) & (row < high)
        piece = jnp.where(keep, pieces[k, core, d].astype(F32), 0.0)
        first, second = piece[:, :, :HALF], piece[:, :, HALF:]
        here = lane >= col_offset
        third_block = jnp.minimum(block + 2, grad.shape[3] // HALF - 1)
        for where_to, value in (
            (block, jnp.where(here, first, 0.0)),
            (block + 1, second),
            (third_block, jnp.where(here, 0.0, first)),
        ):
            cols = pl.ds(pl.multiple_of(where_to * HALF, HALF), HALF)
            grad[0, :, :, cols] = grad[0, :, :, cols] + value
        return carry

    lax.fori_loop(0, 4 * (RIM + 1), add, 0)


def deposit_call(idx_all, pieces, probe_sum, columns):
    vmem_spec = pl.BlockSpec(memory_space=pltpu.VMEM)
    return pl.pallas_call(
        deposit_kernel,
        out_shape=(
            jax.ShapeDtypeStruct((1, 2, STRIP, columns), F32),
            jax.ShapeDtypeStruct(probe_sum.shape, F32),
        ),
        in_specs=[pl.BlockSpec(memory_space=pltpu.SMEM), vmem_spec, vmem_spec],
        out_specs=(vmem_spec, vmem_spec),
        compiler_params=pltpu.CompilerParams(vmem_limit_bytes=62 * 1024 * 1024),
        name="deposit",
    )(idx_all, pieces, probe_sum)


def local(transmission, probe, exit_adjoint, scan_row, scan_col):
    pieces, idx_all, probe_sum = main_call(transmission, probe, exit_adjoint, scan_row, scan_col)
    object_grad, probe_grad = deposit_call(idx_all, pieces, probe_sum, transmission.shape[3])
    return object_grad, probe_grad.reshape(2, STRIP, SIDE)


def solution(mesh):
    placed = (
        P("depth", None, "scan", None),
        P(),
        P(None, "scan", None, None, None),
        P(None, "scan"),
        P(None, "scan"),
    )
    return jax.shard_map(
        local,
        mesh=mesh,
        in_specs=placed,
        out_specs=(P("depth", None, "scan", None), P(None, "depth", None)),
        check_vma=False,
    )
```
